32 devices in a mesh: row: 8 (over z, y), col: 4 (over x, core).
Axes of the slice: x: 2, y: 2, z: 4, core: 2. Of those that a mesh axis runs over, the one named last changes fastest.
Arguments:
- queries: bfloat16 [4096, 1792], P(('row', 'col')), may hold values from -120 to 120, as said below
- keys_values: bfloat16 [4096, 512], P(('row', 'col')), may hold values from -5.5 to 5.5
- segment_ids: int32 [4096], P(('row', 'col')), may hold values from 0 to 7, never falling along the last dimension, each value on 1 to 3072 neighbouring positions
Outputs:
- context: bfloat16 [4096, 1792], P(('row', 'col'))
The draws below stay inside these ranges and needn't reach their ends.
Inputs may be any that keep to these rules, and one draw needn't show every extreme that they name: `queries`: some query rows may be large multiples of a visible key, so scores reach about 270.
All inputs are finite; a program needn't handle non-finite values.
Results may differ from the reference program's by a relative error of at most 0.017.
Values may be sent and summed in bfloat16 or wider, within the bound.
A program may use at most 128 MiB of HBM per device.

```python
import math
import jax
import jax.numpy as jnp
import numpy as np
from jax import lax

HD = 128
KVH = 2
GROUP = 7
TOK_DEV = 128
SEQ = 4096
DOCS = 8
MAXDOC = 3072
N_ROW = 8
N_COL = 4


def draw_pair(key):
    keys = jnp.clip(jax.random.normal(jax.random.fold_in(key, 102), (SEQ, KVH, HD), jnp.float32), -5.0, 5.0)
    values = jnp.clip(jax.random.normal(jax.random.fold_in(key, 103), (SEQ, KVH, HD), jnp.float32), -5.0, 5.0)
    base = jax.random.normal(jax.random.fold_in(key, 101), (SEQ, KVH, GROUP, HD), jnp.float32)
    queries = 2.5 * jnp.clip(base, -5.0, 5.0)
    return (queries, keys, values)


def draw_queries(key, part):
    queries, keys, values = draw_pair(key)
    return queries.reshape(SEQ, KVH * GROUP * HD).astype(jnp.bfloat16)


def draw_keys_values(key, part):
    queries, keys, values = draw_pair(key)
    joined = jnp.concatenate([keys.reshape(SEQ, KVH * HD), values.reshape(SEQ, KVH * HD)], axis=1)
    return joined.astype(jnp.bfloat16)


def profile(number_of, total, limit, skew):
    weights = [(1 << 20) // math.isqrt(rank ** skew) + 1 for rank in range(2, number_of + 1)]
    spare, given = total - limit - (number_of - 1), [1] * (number_of - 1)
    while spare > 0:
        candidates = [i for i in range(number_of - 1) if given[i] < limit]
        pool, left = sum([weights[i] for i in candidates]), spare
        for i in candidates:
            addition = min(limit - given[i], max(1, left * weights[i] // pool), spare)
            given[i] = given[i] + addition
            spare = spare - addition
    return np.array([limit] + given)


def ragged_sizes(own_key, count, total, limit, skew):
    if count == 2:
        one = jax.random.randint(own_key, (), max(1, total - limit), min(limit, total - 1) + 1)
        return jnp.stack([one, total - one])
    lengths = jnp.asarray(profile(count, total, limit, skew), jnp.int32)
    twos = (count - 1) // 2
    source_of, sink = lengths[1:1 + 2 * twos:2], lengths[2:2 + 2 * twos:2]
    room = jnp.minimum(source_of - 1, limit - sink)
    shifted = jax.random.randint(jax.random.fold_in(own_key, 1), (twos,), 0, 1 << 20) % (room + 1)
    lengths = lengths.at[1:1 + 2 * twos:2].set(source_of - shifted).at[2:2 + 2 * twos:2].set(sink + shifted)
    return lengths[jax.random.permutation(jax.random.fold_in(own_key, 2), count)]


def setup_inputs(seed: int = 0) -> dict:
    splits = jax.random.split(jax.random.key(seed), 4)
    return {
        "queries": draw_queries(jax.random.fold_in(splits[3], 71), 0),
        "keys_values": draw_keys_values(jax.random.fold_in(splits[3], 71), 0),
        "segment_ids": jnp.searchsorted(jnp.cumsum(ragged_sizes(splits[2], DOCS, SEQ, MAXDOC, 0)), jnp.arange(SEQ), side="right").astype(jnp.int32),
    }


NEG = -1e+30

def reference(queries, keys_values, segment_ids):
    seq = queries.shape[0]
    slab = N_COL * TOK_DEV
    pad = MAXDOC
    span = pad + slab
    per_col = span // N_COL
    scale = 1.0 / math.sqrt(HD)
    feat = 2 * KVH * HD
    kv_pad = jnp.concatenate([jnp.zeros((pad, feat), keys_values.dtype), keys_values], axis=0)
    seg_pad = jnp.concatenate([jnp.full((pad,), -1, jnp.int32), segment_ids.astype(jnp.int32)], axis=0)
    pos_pad = jnp.arange(seq + pad, dtype=jnp.int32) - jnp.int32(pad)

    def slab_fn(index):
        start = (index * slab).astype(jnp.int32)
        q_rows = lax.dynamic_slice_in_dim(queries, start, slab, 0).astype(jnp.float32)
        q_rows = q_rows.reshape(slab, KVH, GROUP, HD)
        q_pos = start + jnp.arange(slab, dtype=jnp.int32)
        q_seg = lax.dynamic_slice_in_dim(segment_ids.astype(jnp.int32), start, slab, 0)
        kv_win = lax.dynamic_slice_in_dim(kv_pad, start, span, 0)
        seg_win = lax.dynamic_slice_in_dim(seg_pad, start, span, 0)
        pos_win = lax.dynamic_slice_in_dim(pos_pad, start, span, 0)
        kv_cols = kv_win.reshape(span // slab, N_COL, TOK_DEV, feat).transpose(1, 0, 2, 3).reshape(N_COL, per_col, feat)
        seg_cols = seg_win.reshape(span // slab, N_COL, TOK_DEV).transpose(1, 0, 2).reshape(N_COL, per_col)
        pos_cols = pos_win.reshape(span // slab, N_COL, TOK_DEV).transpose(1, 0, 2).reshape(N_COL, per_col)

        def column_fn(args):
            kv_c, seg_c, pos_c = args
            keys = kv_c[:, :KVH * HD].astype(jnp.float32).reshape(per_col, KVH, HD)
            values = kv_c[:, KVH * HD:].astype(jnp.float32).reshape(per_col, KVH, HD)
            visible = (pos_c[None, :] <= q_pos[:, None]) & (seg_c[None, :] == q_seg[:, None])
            shown = visible[:, None, None, :]
            scores = jnp.einsum('qgrd,kgd->qgrk', q_rows, keys) * scale
            scores = jnp.where(shown, scores, NEG)
            top_c = lax.optimization_barrier(jnp.max(scores, axis=-1))
            weights = jnp.where(shown, jnp.exp(scores - top_c[..., None]), 0.0)
            total_c = lax.optimization_barrier(jnp.sum(weights, axis=-1))
            weight_b = lax.optimization_barrier(weights.astype(jnp.bfloat16)).astype(jnp.float32)
            acc_c = jnp.einsum('qgrk,kgd->qgrd', weight_b, values)
            return (top_c, total_c, acc_c)
        top_c, total_c, acc_c = lax.map(column_fn, (kv_cols, seg_cols, pos_cols))
        top = lax.optimization_barrier(jnp.max(top_c, axis=0))
        factor = jnp.exp(top_c - top[None])
        term = lax.optimization_barrier((acc_c * factor[..., None]).astype(jnp.bfloat16)).astype(jnp.float32)
        mass = lax.optimization_barrier((total_c * factor).astype(jnp.bfloat16)).astype(jnp.float32)
        out = lax.optimization_barrier(jnp.sum(term, axis=0)) / lax.optimization_barrier(jnp.sum(mass, axis=0))[..., None]
        return out.reshape(slab, KVH * GROUP * HD).astype(jnp.bfloat16)
    slabs = lax.map(slab_fn, jnp.arange(N_ROW, dtype=jnp.int32))
    return slabs.reshape(seq, KVH * GROUP * HD)
```

```python
import functools
import math

import jax
import jax.numpy as jnp
from jax import lax
from jax.experimental import pallas as pl
from jax.experimental.pallas import tpu as pltpu
from jax.sharding import PartitionSpec as P

HD = 128
KVH = 2
BIG = 2.0**100
MESH = pl.DeviceIdType.MESH


def kernel(Z, Y, X, T, G, q_ref, kv_ref, seg_ref, out_ref, buf, stage, qrecv, qt, bias, mx, tot, acc, ostage,
           pre_send, pre_recv, send, recv, out_send, out_recv):
    KR = T
    SR = T + 16
    row = lax.axis_index("row")
    col = lax.axis_index("col")
    z, y = row // Y, row % Y
    x, c = col // 2, col % 2
    o = 1 - c
    me = row * X + x
    C = 2 * T
    W = G * HD
    NX = X - 1
    scale = math.log2(math.e) / math.sqrt(HD)

    def at(zz, yy, xx):
        return (zz * Y + yy, xx * 2 + c)

    sibling = (row, x * 2 + o)
    up = at(z + 1, y, x)
    side = at(z, 1 - y, x)

    def xnext(dx):
        return lax.rem(x + dx, X)

    def xprev(dx):
        return lax.rem(x - dx + X, X)

    barrier = pltpu.get_barrier_semaphore()
    pl.semaphore_signal(barrier, inc=1, device_id=sibling, device_id_type=MESH)
    pl.semaphore_signal(barrier, inc=1, device_id=side, device_id_type=MESH)
    for dx in range(1, X):
        pl.semaphore_signal(barrier, inc=1, device_id=at(z, y, xnext(dx)), device_id_type=MESH)

    @pl.when(z < Z - 1)
    def _():
        pl.semaphore_signal(barrier, inc=1, device_id=up, device_id_type=MESH)

    @pl.when(z > 0)
    def _():
        pl.semaphore_signal(barrier, inc=1, device_id=at(z - 1, y, x), device_id_type=MESH)

    seg16 = jnp.broadcast_to(seg_ref[...].astype(jnp.float32), (16, T)).astype(jnp.bfloat16)

    def piece(ref, h):
        ref[0:KR, :] = kv_ref[:, pl.ds(pl.multiple_of(h * HD, HD), HD)]
        ref[KR:SR, :] = seg16
        ref[SR:, :] = kv_ref[:, pl.ds(pl.multiple_of((KVH + h) * HD, HD), HD)].T

    piece(stage, o)
    pl.semaphore_wait(
        barrier, 2 + NX + jnp.where(z < Z - 1, 1, 0) + jnp.where(z > 0, 1, 0)
    )

    def remote(src, dst, s_sem, r_sem, device):
        return pltpu.make_async_remote_copy(
            src_ref=src, dst_ref=dst, send_sem=s_sem, recv_sem=r_sem, device_id=device, device_id_type=MESH
        )

    kv_swap = remote(stage, buf.at[me, c], pre_send.at[0], pre_recv.at[0], sibling)
    kv_swap.start()
    q_swap = remote(
        q_ref.at[:, pl.ds(pl.multiple_of(o * W, HD), W)], qrecv, pre_send.at[1], pre_recv.at[1], sibling
    )
    q_swap.start()
    piece(buf.at[me, c], c)
    for g in range(G):
        tile = q_ref[:, pl.ds(pl.multiple_of(c * W + g * HD, HD), HD)].T
        qt[0:HD, pl.ds(pl.multiple_of(g * C + c * T, T), T)] = tile
    remote(stage, buf.at[me, o], pre_send.at[0], pre_recv.at[0], sibling).wait_recv()

    def number(zz, yy, xx):
        return (zz * Y + yy) * X + xx

    def copy(kind, s, block, half, device, r_step=None):
        ref = buf.at[block] if half is None else buf.at[block, half]
        return remote(ref, ref, send.at[s, kind], recv.at[s if r_step is None else r_step, kind], device)

    def send_own(s):
        b = number(z - s, y, x)

        @pl.when(s > 0)
        def _():
            copy(0, s, b, None, up).wait_recv()

        @pl.when(z < Z - 1)
        def _():
            copy(0, s, b, None, up, s + 1).start()

        copy(1, s, b, None, side).start()
        for dx in range(1, X):
            copy(1 + dx, s, b, None, at(z, y, xnext(dx))).start()

    def send_diagonal(s):
        b = number(z - s, 1 - y, x)
        copy(1, s, b, None, side).wait_recv()
        for dx in range(1, X):
            copy(1 + NX + dx, s, b, 0, at(z, y, xnext(dx))).start()
        for dx in range(1, X):
            b = number(z - s, y, xprev(dx))
            copy(1 + dx, s, b, None, side).wait_recv()
            copy(1 + 2 * NX + dx, s, b, 1, side).start()

    send_own(jnp.int32(0))

    q_swap.wait_recv()
    for g in range(G):
        qt[0:HD, pl.ds(pl.multiple_of(g * C + o * T, T), T)] = qrecv[:, g * HD:(g + 1) * HD].T
    seg0 = buf[me, 0, KR:SR, :].astype(jnp.float32)
    seg1 = buf[me, 1, KR:SR, :].astype(jnp.float32)
    first = jnp.min(seg0, axis=1, keepdims=True)
    seg_q = jnp.concatenate([seg0, seg1], axis=1)
    hidden = jnp.where(seg_q == first, 0.0, -BIG)
    rows = lax.broadcasted_iota(jnp.int32, (16, C), 0)
    top16 = jnp.where(rows == 0, -BIG, jnp.where(rows == 1, hidden, 0.0)).astype(jnp.bfloat16)
    for g in range(G):
        qt[HD:HD + 16, g * C:(g + 1) * C] = top16
        qt[HD + 16:, g * C:(g + 1) * C] = jnp.zeros((HD - 16, C), jnp.bfloat16)
    turned = [jnp.broadcast_to(s[0:1, :], (T, T)).T for s in (seg0, seg1)]
    seg_k = jnp.concatenate(turned, axis=0)
    seg_k = jnp.concatenate([seg_k, seg_k], axis=1)
    k_at = lax.broadcasted_iota(jnp.int32, (C, C), 0)
    q_at = lax.broadcasted_iota(jnp.int32, (C, C), 1)
    bias[...] = jnp.where((seg_k == seg_q[0:1, :]) & (k_at <= q_at), 0.0, -BIG)

    def values_of(b):
        return jnp.concatenate([buf[b, 0, SR:, :], buf[b, 1, SR:, :]], axis=1)

    keys = jnp.concatenate([buf[me, 0, 0:KR, :], buf[me, 1, 0:KR, :]], axis=0)
    values = values_of(me)
    for g in range(G):
        score = jnp.dot(keys, qt[0:HD, g * C:(g + 1) * C], preferred_element_type=jnp.float32) + bias[...]
        high = jnp.max(score, axis=0, keepdims=True)
        weight = jnp.exp2((score - high) * scale)
        mx[g] = high
        tot[g] = jnp.sum(weight, axis=0, keepdims=True)
        acc[g] = jnp.dot(values, weight.astype(jnp.bfloat16), preferred_element_type=jnp.float32)

    lane = lax.broadcasted_iota(jnp.int32, (T, HD), 1)
    depth = lax.broadcasted_iota(jnp.int32, (T, HD), 0).astype(jnp.float32)

    def half_keys(b, half):
        seg = buf[b, half, KR:SR, :].astype(jnp.float32)
        shown = jnp.sum(jnp.where(seg == first, 1.0, 0.0), axis=1, keepdims=True)
        masked = jnp.where(depth < T - shown[0:1, :], 1.0, 0.0)
        extra = jnp.where(lane == 0, masked, 1.0).astype(jnp.bfloat16)
        return jnp.concatenate([buf[b, half, 0:KR, :], extra], axis=1)

    def attend(b):
        keys = jnp.concatenate([half_keys(b, 0), half_keys(b, 1)], axis=0)
        values = values_of(b)
        for g in range(G):
            score = jnp.dot(keys, qt[:, g * C:(g + 1) * C], preferred_element_type=jnp.float32)
            old = mx[g]
            high = jnp.maximum(old, jnp.max(score, axis=0, keepdims=True))
            weight = jnp.exp2((score - high) * scale)
            factor = jnp.exp2((old - high) * scale)
            mx[g] = high
            tot[g] = tot[g] * factor + jnp.sum(weight, axis=0, keepdims=True)
            acc[g] = acc[g] * factor + jnp.dot(
                values, weight.astype(jnp.bfloat16), preferred_element_type=jnp.float32
            )

    def step(s, unused):
        @pl.when((s > 0) & (s <= z))
        def _():
            send_own(s)

        def early(j, unused):
            p = s - 1
            b = jnp.where(j == 0, number(z - s, y, x), number(z - p, 1 - y, xprev(j)))
            here = jnp.where(j == 0, s <= z, p <= z) & (s > 0)

            @pl.when(here & (j > 0))
            def _():
                copy(1 + NX + j, p, b, 0, side).wait_recv()
                copy(1 + 2 * NX + j, p, b, 1, side).wait_recv()

            @pl.when(here & (b < me))
            def _():
                attend(b)

            return unused

        lax.fori_loop(0, X, early, 0)

        @pl.when(s <= z)
        def _():
            send_diagonal(s)

        def late(j, unused):
            b = jnp.where(j == 0, number(z - s, 1 - y, x), number(z - s, y, xprev(j)))

            @pl.when((s <= z) & (b < me))
            def _():
                attend(b)

            return unused

        lax.fori_loop(0, X, late, 0)
        return unused

    lax.fori_loop(0, Z + 1, step, 0)

    mine = pl.ds(pl.multiple_of(c * T, T), T)
    theirs = pl.ds(pl.multiple_of(o * T, T), T)
    swaps = []
    for g in range(G):
        place = out_ref.at[:, pl.ds(pl.multiple_of(c * W + g * HD, HD), HD)]
        ostage[g] = (acc[g, :, theirs] / tot[g, :, theirs]).T.astype(jnp.bfloat16)
        swap = remote(ostage.at[g], place, out_send.at[g], out_recv.at[g], sibling)
        swap.start()
        swaps.append(swap)
        place[...] = (acc[g, :, mine] / tot[g, :, mine]).T.astype(jnp.bfloat16)

    def drain(s, unused):
        @pl.when(s <= z)
        def _():
            b = number(z - s, y, x)

            @pl.when(z < Z - 1)
            def _():
                copy(0, s, b, None, up, s + 1).wait_send()

            copy(1, s, b, None, side).wait_send()
            for dx in range(1, X):
                copy(1 + dx, s, b, None, side).wait_send()
                copy(1 + NX + dx, s, b, 0, side).wait_send()
                copy(1 + 2 * NX + dx, s, b, 1, side).wait_send()

        return unused

    kv_swap.wait_send()
    q_swap.wait_send()
    lax.fori_loop(0, Z, drain, 0)
    for g in range(G):
        swaps[g].wait_send()
        place = out_ref.at[:, pl.ds(pl.multiple_of(o * W + g * HD, HD), HD)]
        remote(ostage.at[g], place, out_send.at[g], out_recv.at[g], sibling).wait_recv()


def shards(queries, keys_values, segment_ids, n_row, n_col):
    T = queries.shape[0]
    G = queries.shape[1] // (KVH * HD)
    Y = 2
    Z = n_row // Y
    X = n_col // 2
    chips = Z * Y * X
    kinds = 2 + 3 * (X - 1)
    C = 2 * T
    vmem = pl.BlockSpec(memory_space=pltpu.VMEM)
    dma = pltpu.SemaphoreType.DMA
    return pl.pallas_call(
        functools.partial(kernel, Z, Y, X, T, G),
        out_shape=jax.ShapeDtypeStruct(queries.shape, jnp.bfloat16),
        in_specs=[vmem] * 3,
        out_specs=vmem,
        scratch_shapes=[
            pltpu.VMEM((chips, 2, 2 * T + 16, HD), jnp.bfloat16),
            pltpu.VMEM((2 * T + 16, HD), jnp.bfloat16),
            pltpu.VMEM((T, G * HD), jnp.bfloat16),
            pltpu.VMEM((2 * HD, G * C), jnp.bfloat16),
            pltpu.VMEM((C, C), jnp.float32),
            pltpu.VMEM((G, 1, C), jnp.float32),
            pltpu.VMEM((G, 1, C), jnp.float32),
            pltpu.VMEM((G, HD, C), jnp.float32),
            pltpu.VMEM((G, T, HD), jnp.bfloat16),
            dma((2,)),
            dma((2,)),
            dma((Z, kinds)),
            dma((Z, kinds)),
            dma((G,)),
            dma((G,)),
        ],
        compiler_params=pltpu.CompilerParams(
            collective_id=0, has_side_effects=True, vmem_limit_bytes=48 * 1024 * 1024
        ),
    )(queries, keys_values, segment_ids.reshape(1, T))


def solution(mesh):
    in_specs = (P(("row", "col"), None), P(("row", "col"), None), P(("row", "col")))
    out_specs = P(("row", "col"), None)
    body = functools.partial(shards, n_row=mesh.shape["row"], n_col=mesh.shape["col"])
    return jax.shard_map(body, mesh=mesh, in_specs=in_specs, out_specs=out_specs, check_vma=False)
```

```python
import functools
import math

import jax
import jax.numpy as jnp
from jax import lax
from jax.experimental import pallas as pl
from jax.experimental.pallas import tpu as pltpu
from jax.sharding import PartitionSpec as P

HD = 128
KVH = 2
BIG = 2.0**100
MESH = pl.DeviceIdType.MESH


def kernel(Z, Y, X, T, G, q_hbm, kv_hbm, seg_hbm, out_ref, q_ref, kv_ref, seg_ref, load, buf, stage, qrecv, qt, bias, mx, tot, acc, ostage,
           pre_send, pre_recv, send, recv, out_send, out_recv):
    KR = T
    SR = T + 16
    row = lax.axis_index("row")
    col = lax.axis_index("col")
    z, y = row // Y, row % Y
    x, c = col // 2, col % 2
    o = 1 - c
    me = row * X + x
    C = 2 * T
    W = G * HD
    NX = X - 1
    scale = math.log2(math.e) / math.sqrt(HD)

    def at(zz, yy, xx):
        return (zz * Y + yy, xx * 2 + c)

    sibling = (row, x * 2 + o)
    up = at(z + 1, y, x)
    side = at(z, 1 - y, x)

    def xnext(dx):
        return lax.rem(x + dx, X)

    def xprev(dx):
        return lax.rem(x - dx + X, X)

    q_load = pltpu.make_async_copy(q_hbm.at[:, pl.ds(pl.multiple_of(c * W, HD), W)], q_ref, load.at[0])
    kv_load = pltpu.make_async_copy(kv_hbm, kv_ref, load.at[1])
    seg_load = pltpu.make_async_copy(seg_hbm, seg_ref, load.at[2])
    kv_load.start()
    seg_load.start()
    q_load.start()

    barrier = pltpu.get_barrier_semaphore()
    pl.semaphore_signal(barrier, inc=1, device_id=sibling, device_id_type=MESH)
    pl.semaphore_signal(barrier, inc=1, device_id=side, device_id_type=MESH)
    for dx in range(1, X):
        pl.semaphore_signal(barrier, inc=1, device_id=at(z, y, xnext(dx)), device_id_type=MESH)

    @pl.when(z < Z - 1)
    def _():
        pl.semaphore_signal(barrier, inc=1, device_id=up, device_id_type=MESH)

    @pl.when(z > 0)
    def _():
        pl.semaphore_signal(barrier, inc=1, device_id=at(z - 1, y, x), device_id_type=MESH)

    kv_load.wait()
    seg_load.wait()

    seg16 = jnp.broadcast_to(seg_ref[...].astype(jnp.float32), (16, T)).astype(jnp.bfloat16)

    def piece(ref, h):
        ref[0:KR, :] = kv_ref[:, pl.ds(pl.multiple_of(h * HD, HD), HD)]
        ref[KR:SR, :] = seg16
        ref[SR:, :] = kv_ref[:, pl.ds(pl.multiple_of((KVH + h) * HD, HD), HD)].T

    piece(stage, o)
    pl.semaphore_wait(
        barrier, 2 + NX + jnp.where(z < Z - 1, 1, 0) + jnp.where(z > 0, 1, 0)
    )

    def remote(src, dst, s_sem, r_sem, device):
        return pltpu.make_async_remote_copy(
            src_ref=src, dst_ref=dst, send_sem=s_sem, recv_sem=r_sem, device_id=device, device_id_type=MESH
        )

    kv_swap = remote(stage, buf.at[me, c], pre_send.at[0], pre_recv.at[0], sibling)
    kv_swap.start()
    q_swap = remote(
        q_hbm.at[:, pl.ds(pl.multiple_of(o * W, HD), W)], qrecv, pre_send.at[1], pre_recv.at[1], sibling
    )
    q_swap.start()
    piece(buf.at[me, c], c)
    remote(stage, buf.at[me, o], pre_send.at[0], pre_recv.at[0], sibling).wait_recv()

    def number(zz, yy, xx):
        return (zz * Y + yy) * X + xx

    def copy(kind, s, block, half, device, r_step=None):
        ref = buf.at[block] if half is None else buf.at[block, half]
        return remote(ref, ref, send.at[s, kind], recv.at[s if r_step is None else r_step, kind], device)

    def send_own(s):
        b = number(z - s, y, x)

        @pl.when(s > 0)
        def _():
            copy(0, s, b, None, up).wait_recv()

        @pl.when(z < Z - 1)
        def _():
            copy(0, s, b, None, up, s + 1).start()

        copy(1, s, b, None, side).start()
        for dx in range(1, X):
            copy(1 + dx, s, b, None, at(z, y, xnext(dx))).start()

    def send_diagonal(s):
        b = number(z - s, 1 - y, x)
        copy(1, s, b, None, side).wait_recv()
        for dx in range(1, X):
            copy(1 + NX + dx, s, b, 0, at(z, y, xnext(dx))).start()
        for dx in range(1, X):
            b = number(z - s, y, xprev(dx))
            copy(1 + dx, s, b, None, side).wait_recv()
            copy(1 + 2 * NX + dx, s, b, 1, side).start()

    send_own(jnp.int32(0))

    q_load.wait()
    for g in range(G):
        qt[0:HD, pl.ds(pl.multiple_of(g * C + c * T, T), T)] = q_ref[:, g * HD:(g + 1) * HD].T
    q_swap.wait_recv()
    for g in range(G):
        qt[0:HD, pl.ds(pl.multiple_of(g * C + o * T, T), T)] = qrecv[:, g * HD:(g + 1) * HD].T
    seg0 = buf[me, 0, KR:SR, :].astype(jnp.float32)
    seg1 = buf[me, 1, KR:SR, :].astype(jnp.float32)
    first = jnp.min(seg0, axis=1, keepdims=True)
    seg_q = jnp.concatenate([seg0, seg1], axis=1)
    hidden = jnp.where(seg_q == first, 0.0, -BIG)
    rows = lax.broadcasted_iota(jnp.int32, (16, C), 0)
    top16 = jnp.where(rows == 0, -BIG, jnp.where(rows == 1, hidden, 0.0)).astype(jnp.bfloat16)
    for g in range(G):
        qt[HD:HD + 16, g * C:(g + 1) * C] = top16
        qt[HD + 16:, g * C:(g + 1) * C] = jnp.zeros((HD - 16, C), jnp.bfloat16)
    turned = [jnp.broadcast_to(s[0:1, :], (T, T)).T for s in (seg0, seg1)]
    seg_k = jnp.concatenate(turned, axis=0)
    seg_k = jnp.concatenate([seg_k, seg_k], axis=1)
    k_at = lax.broadcasted_iota(jnp.int32, (C, C), 0)
    q_at = lax.broadcasted_iota(jnp.int32, (C, C), 1)
    bias[...] = jnp.where((seg_k == seg_q[0:1, :]) & (k_at <= q_at), 0.0, -BIG)

    def values_of(b):
        return jnp.concatenate([buf[b, 0, SR:, :], buf[b, 1, SR:, :]], axis=1)

    keys = jnp.concatenate([buf[me, 0, 0:KR, :], buf[me, 1, 0:KR, :]], axis=0)
    values = values_of(me)
    for g in range(G):
        score = jnp.dot(keys, qt[0:HD, g * C:(g + 1) * C], preferred_element_type=jnp.float32) + bias[...]
        high = jnp.max(score, axis=0, keepdims=True)
        weight = jnp.exp2((score - high) * scale)
        mx[g] = high
        tot[g] = jnp.sum(weight, axis=0, keepdims=True)
        acc[g] = jnp.dot(values, weight.astype(jnp.bfloat16), preferred_element_type=jnp.float32)

    lane = lax.broadcasted_iota(jnp.int32, (T, HD), 1)
    depth = lax.broadcasted_iota(jnp.int32, (T, HD), 0).astype(jnp.float32)

    def half_keys(b, half):
        seg = buf[b, half, KR:SR, :].astype(jnp.float32)
        shown = jnp.sum(jnp.where(seg == first, 1.0, 0.0), axis=1, keepdims=True)
        masked = jnp.where(depth < T - shown[0:1, :], 1.0, 0.0)
        extra = jnp.where(lane == 0, masked, 1.0).astype(jnp.bfloat16)
        return jnp.concatenate([buf[b, half, 0:KR, :], extra], axis=1)

    def attend(b):
        keys = jnp.concatenate([half_keys(b, 0), half_keys(b, 1)], axis=0)
        values = values_of(b)
        for g in range(G):
            score = jnp.dot(keys, qt[:, g * C:(g + 1) * C], preferred_element_type=jnp.float32)
            old = mx[g]
            high = jnp.maximum(old, jnp.max(score, axis=0, keepdims=True))
            weight = jnp.exp2((score - high) * scale)
            factor = jnp.exp2((old - high) * scale)
            mx[g] = high
            tot[g] = tot[g] * factor + jnp.sum(weight, axis=0, keepdims=True)
            acc[g] = acc[g] * factor + jnp.dot(
                values, weight.astype(jnp.bfloat16), preferred_element_type=jnp.float32
            )

    def step(s, unused):
        @pl.when((s > 0) & (s <= z))
        def _():
            send_own(s)

        @pl.when((s > 0) & (s - 1 <= z))
        def _():
            send_diagonal(s - 1)

        def blocks(j, unused):
            dx = jnp.where(j < X, j, j - X)
            lag = jnp.where(j == 0, 0, jnp.where(j < X, 2, 1))
            p = s - lag
            diagonal = (j > 0) & (j < X)
            yy = jnp.where(diagonal | (j == X), 1 - y, y)
            b = number(z - p, yy, xprev(dx))
            here = (p >= jnp.where(j == 0, 1, 0)) & (p <= z)

            @pl.when(here & diagonal)
            def _():
                copy(1 + NX + dx, p, b, 0, side).wait_recv()
                copy(1 + 2 * NX + dx, p, b, 1, side).wait_recv()

            @pl.when(here & (b < me))
            def _():
                attend(b)

            return unused

        lax.fori_loop(0, 2 * X, blocks, 0)
        return unused

    lax.fori_loop(0, Z + 2, step, 0)

    mine = pl.ds(pl.multiple_of(c * T, T), T)
    theirs = pl.ds(pl.multiple_of(o * T, T), T)
    swaps = []
    for g in range(G):
        place = out_ref.at[:, pl.ds(pl.multiple_of(c * W + g * HD, HD), HD)]
        ostage[g] = (acc[g, :, theirs] / tot[g, :, theirs]).T.astype(jnp.bfloat16)
        swap = remote(ostage.at[g], place, out_send.at[g], out_recv.at[g], sibling)
        swap.start()
        swaps.append(swap)
        place[...] = (acc[g, :, mine] / tot[g, :, mine]).T.astype(jnp.bfloat16)

    def drain(s, unused):
        @pl.when(s <= z)
        def _():
            b = number(z - s, y, x)

            @pl.when(z < Z - 1)
            def _():
                copy(0, s, b, None, up, s + 1).wait_send()

            copy(1, s, b, None, side).wait_send()
            for dx in range(1, X):
                copy(1 + dx, s, b, None, side).wait_send()
                copy(1 + NX + dx, s, b, 0, side).wait_send()
                copy(1 + 2 * NX + dx, s, b, 1, side).wait_send()

        return unused

    kv_swap.wait_send()
    q_swap.wait_send()
    lax.fori_loop(0, Z, drain, 0)
    for g in range(G):
        swaps[g].wait_send()
        place = out_ref.at[:, pl.ds(pl.multiple_of(o * W + g * HD, HD), HD)]
        remote(ostage.at[g], place, out_send.at[g], out_recv.at[g], sibling).wait_recv()


def shards(queries, keys_values, segment_ids, n_row, n_col):
    T = queries.shape[0]
    G = queries.shape[1] // (KVH * HD)
    Y = 2
    Z = n_row // Y
    X = n_col // 2
    chips = Z * Y * X
    kinds = 2 + 3 * (X - 1)
    C = 2 * T
    vmem = pl.BlockSpec(memory_space=pltpu.VMEM)
    dma = pltpu.SemaphoreType.DMA
    return pl.pallas_call(
        functools.partial(kernel, Z, Y, X, T, G),
        out_shape=jax.ShapeDtypeStruct(queries.shape, jnp.bfloat16),
        in_specs=[pl.BlockSpec(memory_space=pl.ANY)] * 3,
        out_specs=vmem,
        scratch_shapes=[
            pltpu.VMEM((T, G * HD), jnp.bfloat16),
            pltpu.VMEM(keys_values.shape, jnp.bfloat16),
            pltpu.VMEM((1, T), jnp.int32),
            dma((3,)),
            pltpu.VMEM((chips, 2, 2 * T + 16, HD), jnp.bfloat16),
            pltpu.VMEM((2 * T + 16, HD), jnp.bfloat16),
            pltpu.VMEM((T, G * HD), jnp.bfloat16),
            pltpu.VMEM((2 * HD, G * C), jnp.bfloat16),
            pltpu.VMEM((C, C), jnp.float32),
            pltpu.VMEM((G, 1, C), jnp.float32),
            pltpu.VMEM((G, 1, C), jnp.float32),
            pltpu.VMEM((G, HD, C), jnp.float32),
            pltpu.VMEM((G, T, HD), jnp.bfloat16),
            dma((2,)),
            dma((2,)),
            dma((Z, kinds)),
            dma((Z, kinds)),
            dma((G,)),
            dma((G,)),
        ],
        compiler_params=pltpu.CompilerParams(
            collective_id=0, has_side_effects=True, vmem_limit_bytes=60 * 1024 * 1024
        ),
    )(queries, keys_values, segment_ids.reshape(1, T))


def solution(mesh):
    in_specs = (P(("row", "col"), None), P(("row", "col"), None), P(("row", "col")))
    out_specs = P(("row", "col"), None)
    body = functools.partial(shards, n_row=mesh.shape["row"], n_col=mesh.shape["col"])
    return jax.shard_map(body, mesh=mesh, in_specs=in_specs, out_specs=out_specs, check_vma=False)
```

```python
import functools
import math

import jax
import jax.numpy as jnp
from jax import lax
from jax.experimental import pallas as pl
from jax.experimental.pallas import tpu as pltpu
from jax.sharding import PartitionSpec as P

HD = 128
KVH = 2
BIG = 2.0**100
MESH = pl.DeviceIdType.MESH


def kernel(Z, Y, X, T, G, q_hbm, kv_hbm, seg_hbm, out_ref, q_ref, kv_ref, seg_ref, load, buf, stage, qrecv, qt, bias, mx, acc, ostage,
           pre_send, pre_recv, send, recv, out_send, out_recv):
    KR = T
    SR = T + 16
    row = lax.axis_index("row")
    col = lax.axis_index("col")
    z, y = row // Y, row % Y
    x, c = col // 2, col % 2
    o = 1 - c
    me = row * X + x
    C = 2 * T
    W = G * HD
    NX = X - 1
    scale = math.log2(math.e) / math.sqrt(HD)

    def at(zz, yy, xx):
        return (zz * Y + yy, xx * 2 + c)

    sibling = (row, x * 2 + o)
    up = at(z + 1, y, x)
    side = at(z, 1 - y, x)

    def xnext(dx):
        return lax.rem(x + dx, X)

    def xprev(dx):
        return lax.rem(x - dx + X, X)

    q_load = pltpu.make_async_copy(q_hbm.at[:, pl.ds(pl.multiple_of(c * W, HD), W)], q_ref, load.at[0])
    kv_load = pltpu.make_async_copy(kv_hbm, kv_ref, load.at[1])
    seg_load = pltpu.make_async_copy(seg_hbm, seg_ref, load.at[2])
    kv_load.start()
    seg_load.start()
    q_load.start()

    barrier = pltpu.get_barrier_semaphore()
    pl.semaphore_signal(barrier, inc=1, device_id=sibling, device_id_type=MESH)
    pl.semaphore_signal(barrier, inc=1, device_id=side, device_id_type=MESH)
    for dx in range(1, X):
        pl.semaphore_signal(barrier, inc=1, device_id=at(z, y, xnext(dx)), device_id_type=MESH)

    @pl.when(z < Z - 1)
    def _():
        pl.semaphore_signal(barrier, inc=1, device_id=up, device_id_type=MESH)

    @pl.when(z > 0)
    def _():
        pl.semaphore_signal(barrier, inc=1, device_id=at(z - 1, y, x), device_id_type=MESH)

    kv_load.wait()
    seg_load.wait()

    seg16 = jnp.broadcast_to(seg_ref[...].astype(jnp.float32), (16, T)).astype(jnp.bfloat16)

    def piece(ref, h):
        ref[0:KR, :] = kv_ref[:, pl.ds(pl.multiple_of(h * HD, HD), HD)]
        ref[KR:SR, :] = seg16
        ref[SR:, :] = kv_ref[:, pl.ds(pl.multiple_of((KVH + h) * HD, HD), HD)].T

    piece(stage, o)
    pl.semaphore_wait(
        barrier, 2 + NX + jnp.where(z < Z - 1, 1, 0) + jnp.where(z > 0, 1, 0)
    )

    def remote(src, dst, s_sem, r_sem, device):
        return pltpu.make_async_remote_copy(
            src_ref=src, dst_ref=dst, send_sem=s_sem, recv_sem=r_sem, device_id=device, device_id_type=MESH
        )

    kv_swap = remote(stage, buf.at[me, c], pre_send.at[0], pre_recv.at[0], sibling)
    kv_swap.start()
    q_swap = remote(
        q_hbm.at[:, pl.ds(pl.multiple_of(o * W, HD), W)], qrecv, pre_send.at[1], pre_recv.at[1], sibling
    )
    q_swap.start()
    piece(buf.at[me, c], c)
    remote(stage, buf.at[me, o], pre_send.at[0], pre_recv.at[0], sibling).wait_recv()

    def number(zz, yy, xx):
        return (zz * Y + yy) * X + xx

    def copy(kind, s, block, half, device, r_step=None):
        ref = buf.at[block] if half is None else buf.at[block, half]
        return remote(ref, ref, send.at[s, kind], recv.at[s if r_step is None else r_step, kind], device)

    def send_own(s):
        b = number(z - s, y, x)

        @pl.when(s > 0)
        def _():
            copy(0, s, b, None, up).wait_recv()

        @pl.when(z < Z - 1)
        def _():
            copy(0, s, b, None, up, s + 1).start()

        copy(1, s, b, None, side).start()
        for dx in range(1, X):
            copy(1 + dx, s, b, None, at(z, y, xnext(dx))).start()

    def send_diagonal(s):
        b = number(z - s, 1 - y, x)
        copy(1, s, b, None, side).wait_recv()
        for dx in range(1, X):
            copy(1 + NX + dx, s, b, 0, at(z, y, xnext(dx))).start()
        for dx in range(1, X):
            b = number(z - s, y, xprev(dx))
            copy(1 + dx, s, b, None, side).wait_recv()
            copy(1 + 2 * NX + dx, s, b, 1, side).start()

    send_own(jnp.int32(0))

    q_load.wait()
    for g in range(G):
        qt[0:HD, pl.ds(pl.multiple_of(g * C + c * T, T), T)] = q_ref[:, g * HD:(g + 1) * HD].T
    q_swap.wait_recv()
    for g in range(G):
        qt[0:HD, pl.ds(pl.multiple_of(g * C + o * T, T), T)] = qrecv[:, g * HD:(g + 1) * HD].T
    seg0 = buf[me, 0, KR:SR, :].astype(jnp.float32)
    seg1 = buf[me, 1, KR:SR, :].astype(jnp.float32)
    first = jnp.min(seg0, axis=1, keepdims=True)
    seg_q = jnp.concatenate([seg0, seg1], axis=1)
    hidden = jnp.where(seg_q == first, 0.0, -BIG)
    rows = lax.broadcasted_iota(jnp.int32, (16, C), 0)
    top16 = jnp.where(rows == 0, -BIG, jnp.where(rows == 1, hidden, 0.0)).astype(jnp.bfloat16)
    for g in range(G):
        qt[HD:HD + 16, g * C:(g + 1) * C] = top16
        qt[HD + 16:, g * C:(g + 1) * C] = jnp.zeros((HD - 16, C), jnp.bfloat16)
    turned = [jnp.broadcast_to(s[0:1, :], (T, T)).T for s in (seg0, seg1)]
    seg_k = jnp.concatenate(turned, axis=0)
    seg_k = jnp.concatenate([seg_k, seg_k], axis=1)
    k_at = lax.broadcasted_iota(jnp.int32, (C, C), 0)
    q_at = lax.broadcasted_iota(jnp.int32, (C, C), 1)
    bias[...] = jnp.where((seg_k == seg_q[0:1, :]) & (k_at <= q_at), 0.0, -BIG)

    lane = lax.broadcasted_iota(jnp.int32, (T, HD), 1)
    depth = lax.broadcasted_iota(jnp.int32, (T, HD), 0).astype(jnp.float32)

    def half_keys(b, half):
        seg = buf[b, half, KR:SR, :].astype(jnp.float32)
        shown = jnp.sum(jnp.where(seg == first, 1.0, 0.0), axis=1, keepdims=True)
        masked = jnp.where(depth < T - shown[0:1, :], 1.0, 0.0)
        extra = jnp.where(lane == 0, masked, 1.0).astype(jnp.bfloat16)
        return jnp.concatenate([buf[b, half, 0:KR, :], extra], axis=1)

    ones = jnp.ones((16, C), jnp.bfloat16)

    def values_of(b):
        values = jnp.concatenate([buf[b, 0, SR:, :], buf[b, 1, SR:, :]], axis=1)
        return jnp.concatenate([values, ones], axis=0)

    def keys_of(b):
        return jnp.concatenate([half_keys(b, 0), half_keys(b, 1)], axis=0)

    def attend(*blocks):
        keys = jnp.concatenate([keys_of(b) for b in blocks], axis=0)
        values = jnp.concatenate([values_of(b) for b in blocks], axis=1)

        def scores(g):
            return jnp.dot(keys, qt[:, g * C:(g + 1) * C], preferred_element_type=jnp.float32)

        ahead = scores(0)
        for g in range(G):
            score = ahead
            if g + 1 < G:
                ahead = scores(g + 1)
            old = mx[g]
            high = jnp.maximum(old, jnp.max(score, axis=0, keepdims=True))
            weight = jnp.exp2((score - high) * scale).astype(jnp.bfloat16)
            factor = jnp.exp2((old - high) * scale)
            mx[g] = high
            acc[g] = acc[g] * factor + jnp.dot(values, weight, preferred_element_type=jnp.float32)

    keys = jnp.concatenate([buf[me, 0, 0:KR, :], buf[me, 1, 0:KR, :]], axis=0)
    values = values_of(me)

    def own_scores(g):
        return jnp.dot(keys, qt[0:HD, g * C:(g + 1) * C], preferred_element_type=jnp.float32)

    ahead = own_scores(0)
    for g in range(G):
        score = ahead + bias[...]
        if g + 1 < G:
            ahead = own_scores(g + 1)
        high = jnp.max(score, axis=0, keepdims=True)
        weight = jnp.exp2((score - high) * scale).astype(jnp.bfloat16)
        mx[g] = high
        acc[g] = jnp.dot(values, weight, preferred_element_type=jnp.float32)

    def step(s, unused):
        @pl.when((s > 0) & (s <= z))
        def _():
            send_own(s)

        @pl.when((s > 0) & (s - 1 <= z))
        def _():
            send_diagonal(s - 1)

        def entry(j):
            dx = jnp.where(j < X, j, j - X)
            p = s - jnp.where(j == 0, 0, jnp.where(j < X, 2, 1))
            diagonal = (j > 0) & (j < X)
            yy = jnp.where(diagonal | (j == X), 1 - y, y)
            b = number(z - p, yy, xprev(dx))
            here = (p >= jnp.where(j == 0, 1, 0)) & (p <= z)

            @pl.when(here & diagonal)
            def _():
                copy(1 + NX + dx, p, b, 0, side).wait_recv()
                copy(1 + 2 * NX + dx, p, b, 1, side).wait_recv()

            return b, here & (b < me)

        def blocks(j, unused):
            b0, shown0 = entry(2 * j)
            b1, shown1 = entry(2 * j + 1)

            @pl.when(shown0 & shown1)
            def _():
                attend(b0, b1)

            @pl.when(shown0 != shown1)
            def _():
                attend(jnp.where(shown0, b0, b1))

            return unused

        lax.fori_loop(0, X, blocks, 0)
        return unused

    lax.fori_loop(0, Z + 2, step, 0)

    mine = pl.ds(pl.multiple_of(c * T, T), T)
    theirs = pl.ds(pl.multiple_of(o * T, T), T)
    swaps = []
    for g in range(G):
        place = out_ref.at[:, pl.ds(pl.multiple_of(c * W + g * HD, HD), HD)]
        ostage[g] = (acc[g, 0:HD, theirs] / acc[g, HD:HD + 1, theirs]).astype(jnp.bfloat16).T
        swap = remote(ostage.at[g], place, out_send.at[g], out_recv.at[g], sibling)
        swap.start()
        swaps.append(swap)
        place[...] = (acc[g, 0:HD, mine] / acc[g, HD:HD + 1, mine]).astype(jnp.bfloat16).T

    def drain(s, unused):
        @pl.when(s <= z)
        def _():
            b = number(z - s, y, x)

            @pl.when(z < Z - 1)
            def _():
                copy(0, s, b, None, up, s + 1).wait_send()

            copy(1, s, b, None, side).wait_send()
            for dx in range(1, X):
                copy(1 + dx, s, b, None, side).wait_send()
                copy(1 + NX + dx, s, b, 0, side).wait_send()
                copy(1 + 2 * NX + dx, s, b, 1, side).wait_send()

        return unused

    kv_swap.wait_send()
    q_swap.wait_send()
    lax.fori_loop(0, Z, drain, 0)
    for g in range(G):
        swaps[g].wait_send()
        place = out_ref.at[:, pl.ds(pl.multiple_of(o * W + g * HD, HD), HD)]
        remote(ostage.at[g], place, out_send.at[g], out_recv.at[g], sibling).wait_recv()


def shards(queries, keys_values, segment_ids, n_row, n_col):
    T = queries.shape[0]
    G = queries.shape[1] // (KVH * HD)
    Y = 2
    Z = n_row // Y
    X = n_col // 2
    chips = Z * Y * X
    kinds = 2 + 3 * (X - 1)
    C = 2 * T
    vmem = pl.BlockSpec(memory_space=pltpu.VMEM)
    dma = pltpu.SemaphoreType.DMA
    return pl.pallas_call(
        functools.partial(kernel, Z, Y, X, T, G),
        out_shape=jax.ShapeDtypeStruct(queries.shape, jnp.bfloat16),
        in_specs=[pl.BlockSpec(memory_space=pl.ANY)] * 3,
        out_specs=vmem,
        scratch_shapes=[
            pltpu.VMEM((T, G * HD), jnp.bfloat16),
            pltpu.VMEM(keys_values.shape, jnp.bfloat16),
            pltpu.VMEM((1, T), jnp.int32),
            dma((3,)),
            pltpu.VMEM((chips, 2, 2 * T + 16, HD), jnp.bfloat16),
            pltpu.VMEM((2 * T + 16, HD), jnp.bfloat16),
            pltpu.VMEM((T, G * HD), jnp.bfloat16),
            pltpu.VMEM((2 * HD, G * C), jnp.bfloat16),
            pltpu.VMEM((C, C), jnp.float32),
            pltpu.VMEM((G, 1, C), jnp.float32),
            pltpu.VMEM((G, HD + 16, C), jnp.float32),
            pltpu.VMEM((G, T, HD), jnp.bfloat16),
            dma((2,)),
            dma((2,)),
            dma((Z, kinds)),
            dma((Z, kinds)),
            dma((G,)),
            dma((G,)),
        ],
        compiler_params=pltpu.CompilerParams(
            collective_id=0, has_side_effects=True, vmem_limit_bytes=60 * 1024 * 1024
        ),
    )(queries, keys_values, segment_ids.reshape(1, T))


def solution(mesh):
    in_specs = (P(("row", "col"), None), P(("row", "col"), None), P(("row", "col")))
    out_specs = P(("row", "col"), None)
    body = functools.partial(shards, n_row=mesh.shape["row"], n_col=mesh.shape["col"])
    return jax.shard_map(body, mesh=mesh, in_specs=in_specs, out_specs=out_specs, check_vma=False)
```

```python
import functools
import math

import jax
import jax.numpy as jnp
from jax import lax
from jax.experimental import pallas as pl
from jax.experimental.pallas import tpu as pltpu
from jax.sharding import PartitionSpec as P

HD = 128
KVH = 2
BIG = 2.0**100
MESH = pl.DeviceIdType.MESH


def kernel(Z, Y, X, T, G, q_hbm, kv_hbm, seg_hbm, out_ref, q_ref, kv_ref, seg_ref, load, buf, stage, qrecv, qt, bias, mx, acc, ostage,
           pre_send, pre_recv, send, recv, out_send, out_recv):
    KR = T
    SR = T + 16
    row = lax.axis_index("row")
    col = lax.axis_index("col")
    z, y = row // Y, row % Y
    x, c = col // 2, col % 2
    o = 1 - c
    me = row * X + x
    C = 2 * T
    W = G * HD
    NX = X - 1
    reach = 3 * (Z * Y * X) // 4
    scale = math.log2(math.e) / math.sqrt(HD)

    def at(zz, yy, xx):
        return (zz * Y + yy, xx * 2 + c)

    sibling = (row, x * 2 + o)
    up = at(z + 1, y, x)
    side = at(z, 1 - y, x)

    def xnext(dx):
        return lax.rem(x + dx, X)

    def xprev(dx):
        return lax.rem(x - dx + X, X)

    q_load = pltpu.make_async_copy(q_hbm.at[:, pl.ds(pl.multiple_of(c * W, HD), W)], q_ref, load.at[0])
    kv_load = pltpu.make_async_copy(kv_hbm, kv_ref, load.at[1])
    seg_load = pltpu.make_async_copy(seg_hbm, seg_ref, load.at[2])
    kv_load.start()
    seg_load.start()
    q_load.start()

    barrier = pltpu.get_barrier_semaphore()
    pl.semaphore_signal(barrier, inc=1, device_id=sibling, device_id_type=MESH)
    pl.semaphore_signal(barrier, inc=1, device_id=side, device_id_type=MESH)
    for dx in range(1, X):
        pl.semaphore_signal(barrier, inc=1, device_id=at(z, y, xnext(dx)), device_id_type=MESH)

    @pl.when(z < Z - 1)
    def _():
        pl.semaphore_signal(barrier, inc=1, device_id=up, device_id_type=MESH)

    @pl.when(z > 0)
    def _():
        pl.semaphore_signal(barrier, inc=1, device_id=at(z - 1, y, x), device_id_type=MESH)

    kv_load.wait()
    seg_load.wait()

    seg16 = jnp.broadcast_to(seg_ref[...].astype(jnp.float32), (16, T)).astype(jnp.bfloat16)

    def piece(ref, h):
        ref[0:KR, :] = kv_ref[:, pl.ds(pl.multiple_of(h * HD, HD), HD)]
        ref[KR:SR, :] = seg16
        ref[SR:, :] = kv_ref[:, pl.ds(pl.multiple_of((KVH + h) * HD, HD), HD)].T

    piece(stage, o)
    pl.semaphore_wait(
        barrier, 2 + NX + jnp.where(z < Z - 1, 1, 0) + jnp.where(z > 0, 1, 0)
    )

    def remote(src, dst, s_sem, r_sem, device):
        return pltpu.make_async_remote_copy(
            src_ref=src, dst_ref=dst, send_sem=s_sem, recv_sem=r_sem, device_id=device, device_id_type=MESH
        )

    kv_swap = remote(stage, buf.at[me, c], pre_send.at[0], pre_recv.at[0], sibling)
    kv_swap.start()
    q_swap = remote(
        q_hbm.at[:, pl.ds(pl.multiple_of(o * W, HD), W)], qrecv, pre_send.at[1], pre_recv.at[1], sibling
    )
    q_swap.start()
    piece(buf.at[me, c], c)
    remote(stage, buf.at[me, o], pre_send.at[0], pre_recv.at[0], sibling).wait_recv()

    def number(zz, yy, xx):
        return (zz * Y + yy) * X + xx

    def copy(kind, s, block, half, device, r_step=None):
        ref = buf.at[block] if half is None else buf.at[block, half]
        return remote(ref, ref, send.at[s, kind], recv.at[s if r_step is None else r_step, kind], device)

    def need(b, zz, yy, xx):
        i = number(zz, yy, xx)
        return (b < i) & (b >= i - reach)

    def for_row(b, yy):
        start = number(z, yy, 0)
        return (b < start + X - 1) & (b >= start - reach)

    def for_column(b, xx):
        return need(b, z, 0, xx) | need(b, z, 1, xx)

    def for_plane(b, zz):
        return b >= zz * Y * X - reach

    def send_own(s):
        b = number(z - s, y, x)

        @pl.when((s > 0) & for_plane(b, z))
        def _():
            copy(0, s, b, None, up).wait_recv()

        @pl.when((z < Z - 1) & for_plane(b, z + 1))
        def _():
            copy(0, s, b, None, up, s + 1).start()

        @pl.when(for_row(b, 1 - y))
        def _():
            copy(1, s, b, None, side).start()

        for dx in range(1, X):
            @pl.when(for_column(b, xnext(dx)))
            def _():
                copy(1 + dx, s, b, None, at(z, y, xnext(dx))).start()

    def send_diagonal(s):
        b = number(z - s, 1 - y, x)

        @pl.when(for_row(b, y))
        def _():
            copy(1, s, b, None, side).wait_recv()

        for dx in range(1, X):
            @pl.when(need(b, z, y, xnext(dx)))
            def _():
                copy(1 + NX + dx, s, b, 0, at(z, y, xnext(dx))).start()

        for dx in range(1, X):
            e = number(z - s, y, xprev(dx))

            @pl.when(for_column(e, x))
            def _():
                copy(1 + dx, s, e, None, side).wait_recv()

            @pl.when(need(e, z, 1 - y, x))
            def _():
                copy(1 + 2 * NX + dx, s, e, 1, side).start()

    send_own(jnp.int32(0))

    q_load.wait()
    for g in range(G):
        qt[0:HD, pl.ds(pl.multiple_of(g * C + c * T, T), T)] = q_ref[:, g * HD:(g + 1) * HD].T
    q_swap.wait_recv()
    for g in range(G):
        qt[0:HD, pl.ds(pl.multiple_of(g * C + o * T, T), T)] = qrecv[:, g * HD:(g + 1) * HD].T
    seg0 = buf[me, 0, KR:SR, :].astype(jnp.float32)
    seg1 = buf[me, 1, KR:SR, :].astype(jnp.float32)
    first = jnp.min(seg0, axis=1, keepdims=True)
    seg_q = jnp.concatenate([seg0, seg1], axis=1)
    hidden = jnp.where(seg_q == first, 0.0, -BIG)
    rows = lax.broadcasted_iota(jnp.int32, (16, C), 0)
    top16 = jnp.where(rows == 0, -BIG, jnp.where(rows == 1, hidden, 0.0)).astype(jnp.bfloat16)
    for g in range(G):
        qt[HD:HD + 16, g * C:(g + 1) * C] = top16
        qt[HD + 16:, g * C:(g + 1) * C] = jnp.zeros((HD - 16, C), jnp.bfloat16)
    turned = [jnp.broadcast_to(s[0:1, :], (T, T)).T for s in (seg0, seg1)]
    seg_k = jnp.concatenate(turned, axis=0)
    seg_k = jnp.concatenate([seg_k, seg_k], axis=1)
    k_at = lax.broadcasted_iota(jnp.int32, (C, C), 0)
    q_at = lax.broadcasted_iota(jnp.int32, (C, C), 1)
    bias[...] = jnp.where((seg_k == seg_q[0:1, :]) & (k_at <= q_at), 0.0, -BIG)

    lane = lax.broadcasted_iota(jnp.int32, (T, HD), 1)
    depth = lax.broadcasted_iota(jnp.int32, (T, HD), 0).astype(jnp.float32)

    def half_keys(b, half):
        seg = buf[b, half, KR:SR, :].astype(jnp.float32)
        shown = jnp.sum(jnp.where(seg == first, 1.0, 0.0), axis=1, keepdims=True)
        masked = jnp.where(depth < T - shown[0:1, :], 1.0, 0.0)
        extra = jnp.where(lane == 0, masked, 1.0).astype(jnp.bfloat16)
        return jnp.concatenate([buf[b, half, 0:KR, :], extra], axis=1)

    ones = jnp.ones((16, C), jnp.bfloat16)

    def values_of(b):
        values = jnp.concatenate([buf[b, 0, SR:, :], buf[b, 1, SR:, :]], axis=1)
        return jnp.concatenate([values, ones], axis=0)

    def keys_of(b):
        return jnp.concatenate([half_keys(b, 0), half_keys(b, 1)], axis=0)

    def attend(*blocks):
        keys = jnp.concatenate([keys_of(b) for b in blocks], axis=0)
        values = jnp.concatenate([values_of(b) for b in blocks], axis=1)

        def scores(g):
            return jnp.dot(keys, qt[:, g * C:(g + 1) * C], preferred_element_type=jnp.float32)

        ahead = scores(0)
        for g in range(G):
            score = ahead
            if g + 1 < G:
                ahead = scores(g + 1)
            old = mx[g]
            high = jnp.maximum(old, jnp.max(score, axis=0, keepdims=True))
            weight = jnp.exp2((score - high) * scale).astype(jnp.bfloat16)
            factor = jnp.exp2((old - high) * scale)
            mx[g] = high
            acc[g] = acc[g] * factor + jnp.dot(values, weight, preferred_element_type=jnp.float32)

    keys = jnp.concatenate([buf[me, 0, 0:KR, :], buf[me, 1, 0:KR, :]], axis=0)
    values = values_of(me)

    def own_scores(g):
        return jnp.dot(keys, qt[0:HD, g * C:(g + 1) * C], preferred_element_type=jnp.float32)

    ahead = own_scores(0)
    for g in range(G):
        score = ahead + bias[...]
        if g + 1 < G:
            ahead = own_scores(g + 1)
        high = jnp.max(score, axis=0, keepdims=True)
        weight = jnp.exp2((score - high) * scale).astype(jnp.bfloat16)
        mx[g] = high
        acc[g] = jnp.dot(values, weight, preferred_element_type=jnp.float32)

    def step(s, unused):
        @pl.when((s > 0) & (s <= z))
        def _():
            send_own(s)

        @pl.when((s > 0) & (s - 1 <= z))
        def _():
            send_diagonal(s - 1)

        def entry(j):
            dx = jnp.where(j < X, j, j - X)
            p = s - jnp.where(j == 0, 0, jnp.where(j < X, 2, 1))
            diagonal = (j > 0) & (j < X)
            yy = jnp.where(diagonal | (j == X), 1 - y, y)
            b = number(z - p, yy, xprev(dx))
            here = (p >= jnp.where(j == 0, 1, 0)) & (p <= z) & need(b, z, y, x)

            @pl.when(here & diagonal)
            def _():
                copy(1 + NX + dx, p, b, 0, side).wait_recv()
                copy(1 + 2 * NX + dx, p, b, 1, side).wait_recv()

            return b, here

        def blocks(j, unused):
            b0, shown0 = entry(2 * j)
            b1, shown1 = entry(2 * j + 1)

            @pl.when(shown0 & shown1)
            def _():
                attend(b0, b1)

            @pl.when(shown0 != shown1)
            def _():
                attend(jnp.where(shown0, b0, b1))

            return unused

        lax.fori_loop(0, X, blocks, 0)
        return unused

    lax.fori_loop(0, Z + 2, step, 0)

    mine = pl.ds(pl.multiple_of(c * T, T), T)
    theirs = pl.ds(pl.multiple_of(o * T, T), T)
    swaps = []
    for g in range(G):
        place = out_ref.at[:, pl.ds(pl.multiple_of(c * W + g * HD, HD), HD)]
        ostage[g] = (acc[g, 0:HD, theirs] / acc[g, HD:HD + 1, theirs]).astype(jnp.bfloat16).T
        swap = remote(ostage.at[g], place, out_send.at[g], out_recv.at[g], sibling)
        swap.start()
        swaps.append(swap)
        place[...] = (acc[g, 0:HD, mine] / acc[g, HD:HD + 1, mine]).astype(jnp.bfloat16).T

    def drain(s, unused):
        @pl.when(s <= z)
        def _():
            b = number(z - s, y, x)

            @pl.when((z < Z - 1) & for_plane(b, z + 1))
            def _():
                copy(0, s, b, None, up, s + 1).wait_send()

            @pl.when(for_row(b, 1 - y))
            def _():
                copy(1, s, b, None, side).wait_send()

            for dx in range(1, X):
                d = number(z - s, 1 - y, x)
                e = number(z - s, y, xprev(dx))

                @pl.when(for_column(b, xnext(dx)))
                def _():
                    copy(1 + dx, s, b, None, side).wait_send()

                @pl.when(need(d, z, y, xnext(dx)))
                def _():
                    copy(1 + NX + dx, s, d, 0, side).wait_send()

                @pl.when(need(e, z, 1 - y, x))
                def _():
                    copy(1 + 2 * NX + dx, s, e, 1, side).wait_send()

        return unused

    kv_swap.wait_send()
    q_swap.wait_send()
    lax.fori_loop(0, Z, drain, 0)
    for g in range(G):
        swaps[g].wait_send()
        place = out_ref.at[:, pl.ds(pl.multiple_of(o * W + g * HD, HD), HD)]
        remote(ostage.at[g], place, out_send.at[g], out_recv.at[g], sibling).wait_recv()


def shards(queries, keys_values, segment_ids, n_row, n_col):
    T = queries.shape[0]
    G = queries.shape[1] // (KVH * HD)
    Y = 2
    Z = n_row // Y
    X = n_col // 2
    chips = Z * Y * X
    kinds = 2 + 3 * (X - 1)
    C = 2 * T
    vmem = pl.BlockSpec(memory_space=pltpu.VMEM)
    dma = pltpu.SemaphoreType.DMA
    return pl.pallas_call(
        functools.partial(kernel, Z, Y, X, T, G),
        out_shape=jax.ShapeDtypeStruct(queries.shape, jnp.bfloat16),
        in_specs=[pl.BlockSpec(memory_space=pl.ANY)] * 3,
        out_specs=vmem,
        scratch_shapes=[
            pltpu.VMEM((T, G * HD), jnp.bfloat16),
            pltpu.VMEM(keys_values.shape, jnp.bfloat16),
            pltpu.VMEM((1, T), jnp.int32),
            dma((3,)),
            pltpu.VMEM((chips, 2, 2 * T + 16, HD), jnp.bfloat16),
            pltpu.VMEM((2 * T + 16, HD), jnp.bfloat16),
            pltpu.VMEM((T, G * HD), jnp.bfloat16),
            pltpu.VMEM((2 * HD, G * C), jnp.bfloat16),
            pltpu.VMEM((C, C), jnp.float32),
            pltpu.VMEM((G, 1, C), jnp.float32),
            pltpu.VMEM((G, HD + 16, C), jnp.float32),
            pltpu.VMEM((G, T, HD), jnp.bfloat16),
            dma((2,)),
            dma((2,)),
            dma((Z, kinds)),
            dma((Z, kinds)),
            dma((G,)),
            dma((G,)),
        ],
        compiler_params=pltpu.CompilerParams(
            collective_id=0, has_side_effects=True, vmem_limit_bytes=60 * 1024 * 1024
        ),
    )(queries, keys_values, segment_ids.reshape(1, T))


def solution(mesh):
    in_specs = (P(("row", "col"), None), P(("row", "col"), None), P(("row", "col")))
    out_specs = P(("row", "col"), None)
    body = functools.partial(shards, n_row=mesh.shape["row"], n_col=mesh.shape["col"])
    return jax.shard_map(body, mesh=mesh, in_specs=in_specs, out_specs=out_specs, check_vma=False)
```

```python
import functools
import math

import jax
import jax.numpy as jnp
from jax import lax
from jax.experimental import pallas as pl
from jax.experimental.pallas import tpu as pltpu
from jax.sharding import PartitionSpec as P

HD = 128
KVH = 2
BIG = 2.0**100
MESH = pl.DeviceIdType.MESH


def kernel(Z, Y, X, T, G, q_hbm, kv_ref, seg_ref, out_ref, q_ref, load, buf, stage, qrecv, qt, bias, mx, acc, ostage,
           pre_send, pre_recv, send, recv, out_send, out_recv):
    KR = T
    SR = T + 16
    row = lax.axis_index("row")
    col = lax.axis_index("col")
    z, y = row // Y, row % Y
    x, c = col // 2, col % 2
    o = 1 - c
    me = row * X + x
    C = 2 * T
    W = G * HD
    NX = X - 1
    reach = 3 * (Z * Y * X) // 4
    scale = math.log2(math.e) / math.sqrt(HD)

    def at(zz, yy, xx):
        return (zz * Y + yy, xx * 2 + c)

    sibling = (row, x * 2 + o)
    up = at(z + 1, y, x)
    side = at(z, 1 - y, x)

    def xnext(dx):
        return lax.rem(x + dx, X)

    def xprev(dx):
        return lax.rem(x - dx + X, X)

    q_load = pltpu.make_async_copy(q_hbm.at[:, pl.ds(pl.multiple_of(c * W, HD), W)], q_ref, load)
    q_load.start()

    barrier = pltpu.get_barrier_semaphore()
    pl.semaphore_signal(barrier, inc=1, device_id=sibling, device_id_type=MESH)
    pl.semaphore_signal(barrier, inc=1, device_id=side, device_id_type=MESH)
    for dx in range(1, X):
        pl.semaphore_signal(barrier, inc=1, device_id=at(z, y, xnext(dx)), device_id_type=MESH)

    @pl.when(z < Z - 1)
    def _():
        pl.semaphore_signal(barrier, inc=1, device_id=up, device_id_type=MESH)

    @pl.when(z > 0)
    def _():
        pl.semaphore_signal(barrier, inc=1, device_id=at(z - 1, y, x), device_id_type=MESH)

    seg16 = jnp.broadcast_to(seg_ref[...].astype(jnp.float32), (16, T)).astype(jnp.bfloat16)

    def piece(ref, h):
        ref[0:KR, :] = kv_ref[:, pl.ds(pl.multiple_of(h * HD, HD), HD)]
        ref[KR:SR, :] = seg16
        ref[SR:, :] = kv_ref[:, pl.ds(pl.multiple_of((KVH + h) * HD, HD), HD)].T

    piece(stage, o)
    pl.semaphore_wait(
        barrier, 2 + NX + jnp.where(z < Z - 1, 1, 0) + jnp.where(z > 0, 1, 0)
    )

    def remote(src, dst, s_sem, r_sem, device):
        return pltpu.make_async_remote_copy(
            src_ref=src, dst_ref=dst, send_sem=s_sem, recv_sem=r_sem, device_id=device, device_id_type=MESH
        )

    kv_swap = remote(stage, buf.at[me, c], pre_send.at[0], pre_recv.at[0], sibling)
    kv_swap.start()
    q_swap = remote(
        q_hbm.at[:, pl.ds(pl.multiple_of(o * W, HD), W)], qrecv, pre_send.at[1], pre_recv.at[1], sibling
    )
    q_swap.start()
    piece(buf.at[me, c], c)

    def number(zz, yy, xx):
        return (zz * Y + yy) * X + xx

    def along_x(dx, half):
        return 2 + 2 * dx + half

    def onward_x(dx):
        return 3 + 2 * NX + dx

    def onward_y(dx):
        return 3 + 3 * NX + dx

    def copy(kind, s, block, half, device, r_step=None):
        ref = buf.at[block, half]
        return remote(ref, ref, send.at[s, kind], recv.at[s if r_step is None else r_step, kind], device)

    def need(b, zz, yy, xx):
        i = number(zz, yy, xx)
        return (b < i) & (b >= i - reach)

    def for_row(b, yy, half):
        start = number(z, yy, 0)
        return jnp.where(half == 0, (b < start + X - 1) & (b >= start - reach), need(b, z, yy, x))

    def for_column(b, xx, half):
        return need(b, z, y, xx) | (need(b, z, 1 - y, xx) & (half == 1))

    def for_plane(b, zz):
        return b >= zz * Y * X - reach

    def send_half(s, half):
        b = number(z - s, y, x)

        @pl.when((s > 0) & for_plane(b, z))
        def _():
            copy(half, s, b, half, up).wait_recv()

        @pl.when((z < Z - 1) & for_plane(b, z + 1))
        def _():
            copy(half, s, b, half, up, s + 1).start()

        @pl.when(for_row(b, 1 - y, half))
        def _():
            copy(2 + half, s, b, half, side).start()

        for dx in range(1, X):
            @pl.when(for_column(b, xnext(dx), half))
            def _():
                copy(along_x(dx, half), s, b, half, at(z, y, xnext(dx))).start()

    def send_diagonal(s):
        b = number(z - s, 1 - y, x)

        @pl.when(for_row(b, y, 0))
        def _():
            copy(2, s, b, 0, side).wait_recv()

        for dx in range(1, X):
            @pl.when(need(b, z, y, xnext(dx)))
            def _():
                copy(onward_x(dx), s, b, 0, at(z, y, xnext(dx))).start()

        for dx in range(1, X):
            e = number(z - s, y, xprev(dx))

            @pl.when(for_column(e, x, 1))
            def _():
                copy(along_x(dx, 1), s, e, 1, side).wait_recv()

            @pl.when(need(e, z, 1 - y, x))
            def _():
                copy(onward_y(dx), s, e, 1, side).start()

    def relay(s):
        @pl.when(s <= z)
        def _():
            send_half(s, 0)
            send_half(s, 1)

        @pl.when(s - 1 <= z)
        def _():
            send_diagonal(s - 1)

    start = jnp.int32(0)
    send_half(start, c)
    q_load.wait()
    for g in range(G):
        qt[0:HD, pl.ds(pl.multiple_of(g * C + c * T, T), T)] = q_ref[:, g * HD:(g + 1) * HD].T
    remote(stage, buf.at[me, o], pre_send.at[0], pre_recv.at[0], sibling).wait_recv()
    send_half(start, o)

    q_swap.wait_recv()
    for g in range(G):
        qt[0:HD, pl.ds(pl.multiple_of(g * C + o * T, T), T)] = qrecv[:, g * HD:(g + 1) * HD].T
    seg0 = buf[me, 0, KR:SR, :].astype(jnp.float32)
    seg1 = buf[me, 1, KR:SR, :].astype(jnp.float32)
    first = jnp.min(seg0, axis=1, keepdims=True)
    seg_q = jnp.concatenate([seg0, seg1], axis=1)
    hidden = jnp.where(seg_q == first, 0.0, -BIG)
    rows = lax.broadcasted_iota(jnp.int32, (16, C), 0)
    top16 = jnp.where(rows == 0, -BIG, jnp.where(rows == 1, hidden, 0.0)).astype(jnp.bfloat16)
    for g in range(G):
        qt[HD:HD + 16, g * C:(g + 1) * C] = top16
        qt[HD + 16:, g * C:(g + 1) * C] = jnp.zeros((HD - 16, C), jnp.bfloat16)
    turned = [jnp.broadcast_to(s[0:1, :], (T, T)).T for s in (seg0, seg1)]
    seg_k = jnp.concatenate(turned, axis=0)
    seg_k = jnp.concatenate([seg_k, seg_k], axis=1)
    k_at = lax.broadcasted_iota(jnp.int32, (C, C), 0)
    q_at = lax.broadcasted_iota(jnp.int32, (C, C), 1)
    bias[...] = jnp.where((seg_k == seg_q[0:1, :]) & (k_at <= q_at), 0.0, -BIG)

    lane = lax.broadcasted_iota(jnp.int32, (T, HD), 1)
    depth = lax.broadcasted_iota(jnp.int32, (T, HD), 0).astype(jnp.float32)

    def half_keys(b, half):
        seg = buf[b, half, KR:SR, :].astype(jnp.float32)
        shown = jnp.sum(jnp.where(seg == first, 1.0, 0.0), axis=1, keepdims=True)
        masked = jnp.where(depth < T - shown[0:1, :], 1.0, 0.0)
        extra = jnp.where(lane == 0, masked, 1.0).astype(jnp.bfloat16)
        return jnp.concatenate([buf[b, half, 0:KR, :], extra], axis=1)

    ones = jnp.ones((16, C), jnp.bfloat16)

    def values_of(b):
        values = jnp.concatenate([buf[b, 0, SR:, :], buf[b, 1, SR:, :]], axis=1)
        return jnp.concatenate([values, ones], axis=0)

    def keys_of(b):
        return jnp.concatenate([half_keys(b, 0), half_keys(b, 1)], axis=0)

    def attend(*blocks):
        keys = jnp.concatenate([keys_of(b) for b in blocks], axis=0)
        values = jnp.concatenate([values_of(b) for b in blocks], axis=1)

        def scores(g):
            return jnp.dot(keys, qt[:, g * C:(g + 1) * C], preferred_element_type=jnp.float32)

        ahead = scores(0)
        for g in range(G):
            score = ahead
            if g + 1 < G:
                ahead = scores(g + 1)
            old = mx[g]
            high = jnp.maximum(old, jnp.max(score, axis=0, keepdims=True))
            weight = jnp.exp2((score - high) * scale).astype(jnp.bfloat16)
            factor = jnp.exp2((old - high) * scale)
            mx[g] = high
            acc[g] = acc[g] * factor + jnp.dot(values, weight, preferred_element_type=jnp.float32)

    relay(jnp.int32(1))

    keys = jnp.concatenate([buf[me, 0, 0:KR, :], buf[me, 1, 0:KR, :]], axis=0)
    values = values_of(me)

    def own_scores(g):
        return jnp.dot(keys, qt[0:HD, g * C:(g + 1) * C], preferred_element_type=jnp.float32)

    ahead = own_scores(0)
    for g in range(G):
        score = ahead + bias[...]
        if g + 1 < G:
            ahead = own_scores(g + 1)
        high = jnp.max(score, axis=0, keepdims=True)
        weight = jnp.exp2((score - high) * scale).astype(jnp.bfloat16)
        mx[g] = high
        acc[g] = jnp.dot(values, weight, preferred_element_type=jnp.float32)

    def step(s, unused):
        @pl.when(s > 1)
        def _():
            relay(s)

        def entry(j):
            dx = jnp.where(j < X, j, j - X)
            p = s - jnp.where(j == 0, 0, jnp.where(j < X, 2, 1))
            diagonal = (j > 0) & (j < X)
            yy = jnp.where(diagonal | (j == X), 1 - y, y)
            b = number(z - p, yy, xprev(dx))
            here = (p >= jnp.where(j == 0, 1, 0)) & (p <= z) & need(b, z, y, x)

            @pl.when(here & diagonal)
            def _():
                copy(onward_x(dx), p, b, 0, side).wait_recv()
                copy(onward_y(dx), p, b, 1, side).wait_recv()

            @pl.when(here & (j == X))
            def _():
                copy(3, p, b, 1, side).wait_recv()

            @pl.when(here & (j > X))
            def _():
                copy(along_x(dx, 0), p, b, 0, side).wait_recv()

            return b, here

        def blocks(j, unused):
            b0, shown0 = entry(2 * j)
            b1, shown1 = entry(2 * j + 1)

            @pl.when(shown0 & shown1)
            def _():
                attend(b0, b1)

            @pl.when(shown0 != shown1)
            def _():
                attend(jnp.where(shown0, b0, b1))

            return unused

        lax.fori_loop(0, X, blocks, 0)
        return unused

    lax.fori_loop(1, Z + 2, step, 0)

    mine = pl.ds(pl.multiple_of(c * T, T), T)
    theirs = pl.ds(pl.multiple_of(o * T, T), T)
    swaps = []
    for g in range(G):
        place = out_ref.at[:, pl.ds(pl.multiple_of(c * W + g * HD, HD), HD)]
        ostage[g] = (acc[g, 0:HD, theirs] / acc[g, HD:HD + 1, theirs]).astype(jnp.bfloat16).T
        swap = remote(ostage.at[g], place, out_send.at[g], out_recv.at[g], sibling)
        swap.start()
        swaps.append(swap)
        place[...] = (acc[g, 0:HD, mine] / acc[g, HD:HD + 1, mine]).astype(jnp.bfloat16).T

    def drain(s, unused):
        @pl.when(s <= z)
        def _():
            b = number(z - s, y, x)

            for half in range(2):
                @pl.when((z < Z - 1) & for_plane(b, z + 1))
                def _():
                    copy(half, s, b, half, up, s + 1).wait_send()

                @pl.when(for_row(b, 1 - y, half))
                def _():
                    copy(2 + half, s, b, half, side).wait_send()

                for dx in range(1, X):
                    @pl.when(for_column(b, xnext(dx), half))
                    def _():
                        copy(along_x(dx, half), s, b, half, side).wait_send()

            for dx in range(1, X):
                d = number(z - s, 1 - y, x)
                e = number(z - s, y, xprev(dx))

                @pl.when(need(d, z, y, xnext(dx)))
                def _():
                    copy(onward_x(dx), s, d, 0, side).wait_send()

                @pl.when(need(e, z, 1 - y, x))
                def _():
                    copy(onward_y(dx), s, e, 1, side).wait_send()

        return unused

    kv_swap.wait_send()
    q_swap.wait_send()
    lax.fori_loop(0, Z, drain, 0)
    for g in range(G):
        swaps[g].wait_send()
        place = out_ref.at[:, pl.ds(pl.multiple_of(o * W + g * HD, HD), HD)]
        remote(ostage.at[g], place, out_send.at[g], out_recv.at[g], sibling).wait_recv()


def shards(queries, keys_values, segment_ids, n_row, n_col):
    T = queries.shape[0]
    G = queries.shape[1] // (KVH * HD)
    Y = 2
    Z = n_row // Y
    X = n_col // 2
    chips = Z * Y * X
    kinds = 4 + 4 * (X - 1)
    C = 2 * T
    vmem = pl.BlockSpec(memory_space=pltpu.VMEM)
    dma = pltpu.SemaphoreType.DMA
    return pl.pallas_call(
        functools.partial(kernel, Z, Y, X, T, G),
        out_shape=jax.ShapeDtypeStruct(queries.shape, jnp.bfloat16),
        in_specs=[pl.BlockSpec(memory_space=pl.ANY), vmem, vmem],
        out_specs=vmem,
        scratch_shapes=[
            pltpu.VMEM((T, G * HD), jnp.bfloat16),
            dma,
            pltpu.VMEM((chips, 2, 2 * T + 16, HD), jnp.bfloat16),
            pltpu.VMEM((2 * T + 16, HD), jnp.bfloat16),
            pltpu.VMEM((T, G * HD), jnp.bfloat16),
            pltpu.VMEM((2 * HD, G * C), jnp.bfloat16),
            pltpu.VMEM((C, C), jnp.float32),
            pltpu.VMEM((G, 1, C), jnp.float32),
            pltpu.VMEM((G, HD + 16, C), jnp.float32),
            pltpu.VMEM((G, T, HD), jnp.bfloat16),
            dma((2,)),
            dma((2,)),
            dma((Z, kinds)),
            dma((Z, kinds)),
            dma((G,)),
            dma((G,)),
        ],
        compiler_params=pltpu.CompilerParams(
            collective_id=0, has_side_effects=True, vmem_limit_bytes=53 * 1024 * 1024
        ),
    )(queries, keys_values, segment_ids.reshape(1, T))


def solution(mesh):
    in_specs = (P(("row", "col"), None), P(("row", "col"), None), P(("row", "col")))
    out_specs = P(("row", "col"), None)
    body = functools.partial(shards, n_row=mesh.shape["row"], n_col=mesh.shape["col"])
    return jax.shard_map(body, mesh=mesh, in_specs=in_specs, out_specs=out_specs, check_vma=False)
```

```python
import functools
import math

import jax
import jax.numpy as jnp
from jax import lax
from jax.experimental import pallas as pl
from jax.experimental.pallas import tpu as pltpu
from jax.sharding import PartitionSpec as P

HD = 128
KVH = 2
BIG = 2.0**100
MESH = pl.DeviceIdType.MESH


def kernel(Z, Y, X, T, G, q_hbm, kv_ref, seg_ref, out_ref, q_ref, load, buf, stage, qrecv, qt, bias, mx, acc, ostage,
           pre_send, pre_recv, send, recv, out_send, out_recv):
    KR = T
    SR = T + 16
    row = lax.axis_index("row")
    col = lax.axis_index("col")
    z, y = row // Y, row % Y
    x, c = col // 2, col % 2
    o = 1 - c
    me = row * X + x
    C = 2 * T
    W = G * HD
    NX = X - 1
    reach = 3 * (Z * Y * X) // 4
    scale = math.log2(math.e) / math.sqrt(HD)

    def at(zz, yy, xx):
        return (zz * Y + yy, xx * 2 + c)

    sibling = (row, x * 2 + o)
    up = at(z + 1, y, x)
    side = at(z, 1 - y, x)

    def xnext(dx):
        return lax.rem(x + dx, X)

    def xprev(dx):
        return lax.rem(x - dx + X, X)

    q_load = pltpu.make_async_copy(q_hbm.at[:, pl.ds(pl.multiple_of(c * W, HD), W)], q_ref, load)
    q_load.start()

    barrier = pltpu.get_barrier_semaphore()
    pl.semaphore_signal(barrier, inc=1, device_id=sibling, device_id_type=MESH)
    pl.semaphore_signal(barrier, inc=1, device_id=side, device_id_type=MESH)
    for dx in range(1, X):
        pl.semaphore_signal(barrier, inc=1, device_id=at(z, y, xnext(dx)), device_id_type=MESH)

    @pl.when(z < Z - 1)
    def _():
        pl.semaphore_signal(barrier, inc=1, device_id=up, device_id_type=MESH)

    @pl.when(z > 0)
    def _():
        pl.semaphore_signal(barrier, inc=1, device_id=at(z - 1, y, x), device_id_type=MESH)

    seg16 = jnp.broadcast_to(seg_ref[...].astype(jnp.float32), (16, T)).astype(jnp.bfloat16)

    def piece(ref, h):
        ref[0:KR, :] = kv_ref[:, pl.ds(pl.multiple_of(h * HD, HD), HD)]
        ref[KR:SR, :] = seg16
        ref[SR:, :] = kv_ref[:, pl.ds(pl.multiple_of((KVH + h) * HD, HD), HD)].T

    piece(stage, o)
    pl.semaphore_wait(
        barrier, 2 + NX + jnp.where(z < Z - 1, 1, 0) + jnp.where(z > 0, 1, 0)
    )

    def remote(src, dst, s_sem, r_sem, device):
        return pltpu.make_async_remote_copy(
            src_ref=src, dst_ref=dst, send_sem=s_sem, recv_sem=r_sem, device_id=device, device_id_type=MESH
        )

    kv_swap = remote(stage, buf.at[me, c], pre_send.at[0], pre_recv.at[0], sibling)
    kv_swap.start()
    q_swap = remote(
        q_hbm.at[:, pl.ds(pl.multiple_of(o * W, HD), W)], qrecv, pre_send.at[1], pre_recv.at[1], sibling
    )
    q_swap.start()
    piece(buf.at[me, c], c)

    def number(zz, yy, xx):
        return (zz * Y + yy) * X + xx

    def along_x(dx, half):
        return 2 + 2 * dx + half

    def onward_x(dx):
        return 3 + 2 * NX + dx

    def onward_y(dx):
        return 3 + 3 * NX + dx

    def copy(kind, s, block, half, device, r_step=None):
        ref = buf.at[block, half]
        return remote(ref, ref, send.at[s, kind], recv.at[s if r_step is None else r_step, kind], device)

    def need(b, zz, yy, xx):
        i = number(zz, yy, xx)
        return (b < i) & (b >= i - reach)

    def for_row(b, yy, half):
        start = number(z, yy, 0)
        return jnp.where(half == 0, (b < start + X - 1) & (b >= start - reach), need(b, z, yy, x))

    def for_column(b, xx, half):
        return need(b, z, y, xx) | (need(b, z, 1 - y, xx) & (half == 1))

    def for_plane(b, zz):
        return b >= zz * Y * X - reach

    def send_half(s, half):
        b = number(z - s, y, x)

        @pl.when((s > 0) & for_plane(b, z))
        def _():
            copy(half, s, b, half, up).wait_recv()

        @pl.when((z < Z - 1) & for_plane(b, z + 1))
        def _():
            copy(half, s, b, half, up, s + 1).start()

        @pl.when(for_row(b, 1 - y, half))
        def _():
            copy(2 + half, s, b, half, side).start()

        for dx in range(1, X):
            @pl.when(for_column(b, xnext(dx), half))
            def _():
                copy(along_x(dx, half), s, b, half, at(z, y, xnext(dx))).start()

    def send_diagonal(s):
        b = number(z - s, 1 - y, x)

        @pl.when(for_row(b, y, 0))
        def _():
            copy(2, s, b, 0, side).wait_recv()

        for dx in range(1, X):
            @pl.when(need(b, z, y, xnext(dx)))
            def _():
                copy(onward_x(dx), s, b, 0, at(z, y, xnext(dx))).start()

        for dx in range(1, X):
            e = number(z - s, y, xprev(dx))

            @pl.when(for_column(e, x, 1))
            def _():
                copy(along_x(dx, 1), s, e, 1, side).wait_recv()

            @pl.when(need(e, z, 1 - y, x))
            def _():
                copy(onward_y(dx), s, e, 1, side).start()

    def relay(s):
        @pl.when(s <= z)
        def _():
            send_half(s, 0)
            send_half(s, 1)

        @pl.when(s - 1 <= z)
        def _():
            send_diagonal(s - 1)

    start = jnp.int32(0)
    send_half(start, c)
    q_load.wait()
    for g in range(G):
        qt[0:HD, pl.ds(pl.multiple_of(g * C + c * T, T), T)] = q_ref[:, g * HD:(g + 1) * HD].T
    remote(stage, buf.at[me, o], pre_send.at[0], pre_recv.at[0], sibling).wait_recv()
    send_half(start, o)

    q_swap.wait_recv()
    for g in range(G):
        qt[0:HD, pl.ds(pl.multiple_of(g * C + o * T, T), T)] = qrecv[:, g * HD:(g + 1) * HD].T
    seg0 = buf[me, 0, KR:SR, :].astype(jnp.float32)
    seg1 = buf[me, 1, KR:SR, :].astype(jnp.float32)
    first = jnp.min(seg0, axis=1, keepdims=True)
    seg_q = jnp.concatenate([seg0, seg1], axis=1)
    hidden = jnp.where(seg_q == first, 0.0, -BIG)
    rows = lax.broadcasted_iota(jnp.int32, (16, C), 0)
    top16 = jnp.where(rows == 0, -BIG, jnp.where(rows == 1, hidden, 0.0)).astype(jnp.bfloat16)
    for g in range(G):
        qt[HD:HD + 16, g * C:(g + 1) * C] = top16
        qt[HD + 16:, g * C:(g + 1) * C] = jnp.zeros((HD - 16, C), jnp.bfloat16)
    turned = [jnp.broadcast_to(s[0:1, :], (T, T)).T for s in (seg0, seg1)]
    seg_k = jnp.concatenate(turned, axis=0)
    seg_k = jnp.concatenate([seg_k, seg_k], axis=1)
    k_at = lax.broadcasted_iota(jnp.int32, (C, C), 0)
    q_at = lax.broadcasted_iota(jnp.int32, (C, C), 1)
    bias[...] = jnp.where((seg_k == seg_q[0:1, :]) & (k_at <= q_at), 0.0, -BIG)

    lane = lax.broadcasted_iota(jnp.int32, (T, HD), 1)
    depth = lax.broadcasted_iota(jnp.int32, (T, HD), 0).astype(jnp.float32)

    def half_keys(b, half):
        seg = buf[b, half, KR:SR, :].astype(jnp.float32)
        shown = jnp.sum(jnp.where(seg == first, 1.0, 0.0), axis=1, keepdims=True)
        masked = jnp.where(depth < T - shown[0:1, :], 1.0, 0.0)
        extra = jnp.where(lane == 0, masked, 1.0).astype(jnp.bfloat16)
        return jnp.concatenate([buf[b, half, 0:KR, :], extra], axis=1)

    ones = jnp.ones((16, C), jnp.bfloat16)

    def values_of(b):
        values = jnp.concatenate([buf[b, 0, SR:, :], buf[b, 1, SR:, :]], axis=1)
        return jnp.concatenate([values, ones], axis=0)

    def keys_of(b):
        return jnp.concatenate([half_keys(b, 0), half_keys(b, 1)], axis=0)

    def attend(*blocks):
        keys = jnp.concatenate([keys_of(b) for b in blocks], axis=0)
        values = jnp.concatenate([values_of(b) for b in blocks], axis=1)

        def scores(g):
            return jnp.dot(keys, qt[:, g * C:(g + 1) * C], preferred_element_type=jnp.float32)

        def finish(g, factor, weight):
            acc[g] = acc[g] * factor + jnp.dot(values, weight, preferred_element_type=jnp.float32)

        ahead = scores(0)
        behind = None
        for g in range(G):
            score = ahead
            if g + 1 < G:
                ahead = scores(g + 1)
            old = mx[g]
            high = jnp.maximum(old, jnp.max(score, axis=0, keepdims=True))
            weight = jnp.exp2(((score - high) * scale).astype(jnp.bfloat16))
            factor = jnp.exp2((old - high) * scale)
            mx[g] = high
            if behind is not None:
                finish(*behind)
            behind = (g, factor, weight)
        finish(*behind)

    relay(jnp.int32(1))

    keys = jnp.concatenate([buf[me, 0, 0:KR, :], buf[me, 1, 0:KR, :]], axis=0)
    values = values_of(me)

    def own_scores(g):
        return jnp.dot(keys, qt[0:HD, g * C:(g + 1) * C], preferred_element_type=jnp.float32)

    ahead = own_scores(0)
    for g in range(G):
        score = ahead + bias[...]
        if g + 1 < G:
            ahead = own_scores(g + 1)
        high = jnp.max(score, axis=0, keepdims=True)
        weight = jnp.exp2(((score - high) * scale).astype(jnp.bfloat16))
        mx[g] = high
        acc[g] = jnp.dot(values, weight, preferred_element_type=jnp.float32)

    def step(s, unused):
        @pl.when(s > 1)
        def _():
            relay(s)

        def entry(j):
            dx = jnp.where(j < X, j, j - X)
            p = s - jnp.where(j == 0, 0, jnp.where(j < X, 2, 1))
            diagonal = (j > 0) & (j < X)
            yy = jnp.where(diagonal | (j == X), 1 - y, y)
            b = number(z - p, yy, xprev(dx))
            here = (p >= jnp.where(j == 0, 1, 0)) & (p <= z) & need(b, z, y, x)

            @pl.when(here & diagonal)
            def _():
                copy(onward_x(dx), p, b, 0, side).wait_recv()
                copy(onward_y(dx), p, b, 1, side).wait_recv()

            @pl.when(here & (j == X))
            def _():
                copy(3, p, b, 1, side).wait_recv()

            @pl.when(here & (j > X))
            def _():
                copy(along_x(dx, 0), p, b, 0, side).wait_recv()

            return b, here

        def blocks(j, unused):
            b0, shown0 = entry(2 * j)
            b1, shown1 = entry(2 * j + 1)

            @pl.when(shown0 & shown1)
            def _():
                attend(b0, b1)

            @pl.when(shown0 != shown1)
            def _():
                attend(jnp.where(shown0, b0, b1))

            return unused

        lax.fori_loop(0, X, blocks, 0)
        return unused

    lax.fori_loop(1, Z + 2, step, 0)

    mine = pl.ds(pl.multiple_of(c * T, T), T)
    theirs = pl.ds(pl.multiple_of(o * T, T), T)
    swaps = []
    for g in range(G):
        place = out_ref.at[:, pl.ds(pl.multiple_of(c * W + g * HD, HD), HD)]
        ostage[g] = (acc[g, 0:HD, theirs] / acc[g, HD:HD + 1, theirs]).astype(jnp.bfloat16).T
        swap = remote(ostage.at[g], place, out_send.at[g], out_recv.at[g], sibling)
        swap.start()
        swaps.append(swap)
        place[...] = (acc[g, 0:HD, mine] / acc[g, HD:HD + 1, mine]).astype(jnp.bfloat16).T

    def drain(s, unused):
        @pl.when(s <= z)
        def _():
            b = number(z - s, y, x)

            for half in range(2):
                @pl.when((z < Z - 1) & for_plane(b, z + 1))
                def _():
                    copy(half, s, b, half, up, s + 1).wait_send()

                @pl.when(for_row(b, 1 - y, half))
                def _():
                    copy(2 + half, s, b, half, side).wait_send()

                for dx in range(1, X):
                    @pl.when(for_column(b, xnext(dx), half))
                    def _():
                        copy(along_x(dx, half), s, b, half, side).wait_send()

            for dx in range(1, X):
                d = number(z - s, 1 - y, x)
                e = number(z - s, y, xprev(dx))

                @pl.when(need(d, z, y, xnext(dx)))
                def _():
                    copy(onward_x(dx), s, d, 0, side).wait_send()

                @pl.when(need(e, z, 1 - y, x))
                def _():
                    copy(onward_y(dx), s, e, 1, side).wait_send()

        return unused

    kv_swap.wait_send()
    q_swap.wait_send()
    lax.fori_loop(0, Z, drain, 0)
    for g in range(G):
        swaps[g].wait_send()
        place = out_ref.at[:, pl.ds(pl.multiple_of(o * W + g * HD, HD), HD)]
        remote(ostage.at[g], place, out_send.at[g], out_recv.at[g], sibling).wait_recv()


def shards(queries, keys_values, segment_ids, n_row, n_col):
    T = queries.shape[0]
    G = queries.shape[1] // (KVH * HD)
    Y = 2
    Z = n_row // Y
    X = n_col // 2
    chips = Z * Y * X
    kinds = 4 + 4 * (X - 1)
    C = 2 * T
    vmem = pl.BlockSpec(memory_space=pltpu.VMEM)
    dma = pltpu.SemaphoreType.DMA
    return pl.pallas_call(
        functools.partial(kernel, Z, Y, X, T, G),
        out_shape=jax.ShapeDtypeStruct(queries.shape, jnp.bfloat16),
        in_specs=[pl.BlockSpec(memory_space=pl.ANY), vmem, vmem],
        out_specs=vmem,
        scratch_shapes=[
            pltpu.VMEM((T, G * HD), jnp.bfloat16),
            dma,
            pltpu.VMEM((chips, 2, 2 * T + 16, HD), jnp.bfloat16),
            pltpu.VMEM((2 * T + 16, HD), jnp.bfloat16),
            pltpu.VMEM((T, G * HD), jnp.bfloat16),
            pltpu.VMEM((2 * HD, G * C), jnp.bfloat16),
            pltpu.VMEM((C, C), jnp.float32),
            pltpu.VMEM((G, 1, C), jnp.float32),
            pltpu.VMEM((G, HD + 16, C), jnp.float32),
            pltpu.VMEM((G, T, HD), jnp.bfloat16),
            dma((2,)),
            dma((2,)),
            dma((Z, kinds)),
            dma((Z, kinds)),
            dma((G,)),
            dma((G,)),
        ],
        compiler_params=pltpu.CompilerParams(
            collective_id=0, has_side_effects=True, vmem_limit_bytes=53 * 1024 * 1024
        ),
    )(queries, keys_values, segment_ids.reshape(1, T))


def solution(mesh):
    in_specs = (P(("row", "col"), None), P(("row", "col"), None), P(("row", "col")))
    out_specs = P(("row", "col"), None)
    body = functools.partial(shards, n_row=mesh.shape["row"], n_col=mesh.shape["col"])
    return jax.shard_map(body, mesh=mesh, in_specs=in_specs, out_specs=out_specs, check_vma=False)
```

```python
import functools
import math

import jax
import jax.numpy as jnp
from jax import lax
from jax.experimental import pallas as pl
from jax.experimental.pallas import tpu as pltpu
from jax.sharding import PartitionSpec as P

HD = 128
KVH = 2
BIG = 2.0**100
MESH = pl.DeviceIdType.MESH


def kernel(Z, Y, X, T, G, q_hbm, kv_ref, seg_ref, out_ref, q_ref, load, buf, stage, qrecv, qt, bias, mx, acc, ostage,
           pre_send, pre_recv, send, recv, out_send, out_recv):
    KR = T
    SR = T + 16
    row = lax.axis_index("row")
    col = lax.axis_index("col")
    z, y = row // Y, row % Y
    x, c = col // 2, col % 2
    o = 1 - c
    me = row * X + x
    C = 2 * T
    W = G * HD
    NX = X - 1
    reach = 3 * (Z * Y * X) // 4
    scale = math.log2(math.e) / math.sqrt(HD)

    def at(zz, yy, xx):
        return (zz * Y + yy, xx * 2 + c)

    sibling = (row, x * 2 + o)
    up = at(z + 1, y, x)
    side = at(z, 1 - y, x)

    def xnext(dx):
        return lax.rem(x + dx, X)

    def xprev(dx):
        return lax.rem(x - dx + X, X)

    q_load = pltpu.make_async_copy(q_hbm.at[:, pl.ds(pl.multiple_of(c * W, HD), W)], q_ref, load)
    q_load.start()

    barrier = pltpu.get_barrier_semaphore()
    pl.semaphore_signal(barrier, inc=1, device_id=sibling, device_id_type=MESH)
    pl.semaphore_signal(barrier, inc=1, device_id=side, device_id_type=MESH)
    for dx in range(1, X):
        pl.semaphore_signal(barrier, inc=1, device_id=at(z, y, xnext(dx)), device_id_type=MESH)

    @pl.when(z < Z - 1)
    def _():
        pl.semaphore_signal(barrier, inc=1, device_id=up, device_id_type=MESH)

    @pl.when(z > 0)
    def _():
        pl.semaphore_signal(barrier, inc=1, device_id=at(z - 1, y, x), device_id_type=MESH)

    seg16 = jnp.broadcast_to(seg_ref[...].astype(jnp.float32), (16, T)).astype(jnp.bfloat16)

    def piece(ref, h):
        ref[0:KR, :] = kv_ref[:, pl.ds(pl.multiple_of(h * HD, HD), HD)]
        ref[KR:SR, :] = seg16
        ref[SR:, :] = kv_ref[:, pl.ds(pl.multiple_of((KVH + h) * HD, HD), HD)].T

    piece(stage, o)
    pl.semaphore_wait(
        barrier, 2 + NX + jnp.where(z < Z - 1, 1, 0) + jnp.where(z > 0, 1, 0)
    )

    def remote(src, dst, s_sem, r_sem, device):
        return pltpu.make_async_remote_copy(
            src_ref=src, dst_ref=dst, send_sem=s_sem, recv_sem=r_sem, device_id=device, device_id_type=MESH
        )

    kv_swap = remote(stage, buf.at[me, c], pre_send.at[0], pre_recv.at[0], sibling)
    kv_swap.start()
    q_swap = remote(
        q_hbm.at[:, pl.ds(pl.multiple_of(o * W, HD), W)], qrecv, pre_send.at[1], pre_recv.at[1], sibling
    )
    q_swap.start()
    piece(buf.at[me, c], c)

    def number(zz, yy, xx):
        return (zz * Y + yy) * X + xx

    def along_x(dx, half):
        return 2 + 2 * dx + half

    def onward_x(dx):
        return 3 + 2 * NX + dx

    def onward_y(dx):
        return 3 + 3 * NX + dx

    def copy(kind, s, block, half, device, r_step=None):
        ref = buf.at[block, half]
        return remote(ref, ref, send.at[s, kind], recv.at[s if r_step is None else r_step, kind], device)

    def need(b, zz, yy, xx):
        i = number(zz, yy, xx)
        return (b < i) & (b >= i - reach)

    def for_row(b, yy, half):
        start = number(z, yy, 0)
        return jnp.where(half == 0, (b < start + X - 1) & (b >= start - reach), need(b, z, yy, x))

    def for_column(b, xx, half):
        return need(b, z, y, xx) | (need(b, z, 1 - y, xx) & (half == 1))

    def for_plane(b, zz):
        return b >= zz * Y * X - reach

    def send_half(s, half):
        b = number(z - s, y, x)

        @pl.when((s > 0) & for_plane(b, z))
        def _():
            copy(half, s, b, half, up).wait_recv()

        @pl.when((z < Z - 1) & for_plane(b, z + 1))
        def _():
            copy(half, s, b, half, up, s + 1).start()

        @pl.when(for_row(b, 1 - y, half))
        def _():
            copy(2 + half, s, b, half, side).start()

        for dx in range(1, X):
            @pl.when(for_column(b, xnext(dx), half))
            def _():
                copy(along_x(dx, half), s, b, half, at(z, y, xnext(dx))).start()

    def send_diagonal(s):
        b = number(z - s, 1 - y, x)

        @pl.when(for_row(b, y, 0))
        def _():
            copy(2, s, b, 0, side).wait_recv()

        for dx in range(1, X):
            @pl.when(need(b, z, y, xnext(dx)))
            def _():
                copy(onward_x(dx), s, b, 0, at(z, y, xnext(dx))).start()

        for dx in range(1, X):
            e = number(z - s, y, xprev(dx))

            @pl.when(for_column(e, x, 1))
            def _():
                copy(along_x(dx, 1), s, e, 1, side).wait_recv()

            @pl.when(need(e, z, 1 - y, x))
            def _():
                copy(onward_y(dx), s, e, 1, side).start()

    def pass_up(s):
        @pl.when(s <= z)
        def _():
            send_half(s, 0)
            send_half(s, 1)

    def pass_on(s):
        @pl.when(s <= z)
        def _():
            send_diagonal(s)

    start = jnp.int32(0)
    send_half(start, c)
    q_load.wait()
    for g in range(G):
        qt[0:HD, pl.ds(pl.multiple_of(g * C + c * T, T), T)] = q_ref[:, g * HD:(g + 1) * HD].T
    remote(stage, buf.at[me, o], pre_send.at[0], pre_recv.at[0], sibling).wait_recv()
    send_half(start, o)

    q_swap.wait_recv()
    for g in range(G):
        qt[0:HD, pl.ds(pl.multiple_of(g * C + o * T, T), T)] = qrecv[:, g * HD:(g + 1) * HD].T
    seg0 = buf[me, 0, KR:SR, :].astype(jnp.float32)
    seg1 = buf[me, 1, KR:SR, :].astype(jnp.float32)
    first = jnp.min(seg0, axis=1, keepdims=True)
    seg_q = jnp.concatenate([seg0, seg1], axis=1)
    hidden = jnp.where(seg_q == first, 0.0, -BIG)
    rows = lax.broadcasted_iota(jnp.int32, (16, C), 0)
    top16 = jnp.where(rows == 0, -BIG, jnp.where(rows == 1, hidden, 0.0)).astype(jnp.bfloat16)
    for g in range(G):
        qt[HD:HD + 16, g * C:(g + 1) * C] = top16
        qt[HD + 16:, g * C:(g + 1) * C] = jnp.zeros((HD - 16, C), jnp.bfloat16)
    turned = [jnp.broadcast_to(s[0:1, :], (T, T)).T for s in (seg0, seg1)]
    seg_k = jnp.concatenate(turned, axis=0)
    seg_k = jnp.concatenate([seg_k, seg_k], axis=1)
    k_at = lax.broadcasted_iota(jnp.int32, (C, C), 0)
    q_at = lax.broadcasted_iota(jnp.int32, (C, C), 1)
    bias[...] = jnp.where((seg_k == seg_q[0:1, :]) & (k_at <= q_at), 0.0, -BIG)

    lane = lax.broadcasted_iota(jnp.int32, (T, HD), 1)
    depth = lax.broadcasted_iota(jnp.int32, (T, HD), 0).astype(jnp.float32)

    def half_keys(b, half):
        seg = buf[b, half, KR:SR, :].astype(jnp.float32)
        shown = jnp.sum(jnp.where(seg == first, 1.0, 0.0), axis=1, keepdims=True)
        masked = jnp.where(depth < T - shown[0:1, :], 1.0, 0.0)
        extra = jnp.where(lane == 0, masked, 1.0).astype(jnp.bfloat16)
        return jnp.concatenate([buf[b, half, 0:KR, :], extra], axis=1)

    ones = jnp.ones((16, C), jnp.bfloat16)

    def values_of(b):
        values = jnp.concatenate([buf[b, 0, SR:, :], buf[b, 1, SR:, :]], axis=1)
        return jnp.concatenate([values, ones], axis=0)

    def keys_of(b):
        return jnp.concatenate([half_keys(b, 0), half_keys(b, 1)], axis=0)

    def attend(*blocks):
        keys = jnp.concatenate([keys_of(b) for b in blocks], axis=0)
        values = jnp.concatenate([values_of(b) for b in blocks], axis=1)

        def scores(g):
            return jnp.dot(keys, qt[:, g * C:(g + 1) * C], preferred_element_type=jnp.float32)

        def finish(g, factor, weight):
            acc[g] = acc[g] * factor + jnp.dot(values, weight, preferred_element_type=jnp.float32)

        ahead = scores(0)
        behind = None
        for g in range(G):
            score = ahead
            if g + 1 < G:
                ahead = scores(g + 1)
            old = mx[g]
            high = jnp.maximum(old, jnp.max(score, axis=0, keepdims=True))
            weight = jnp.exp2(((score - high) * scale).astype(jnp.bfloat16))
            factor = jnp.exp2((old - high) * scale)
            mx[g] = high
            if behind is not None:
                finish(*behind)
            behind = (g, factor, weight)
        finish(*behind)

    pass_up(jnp.int32(1))
    pass_on(start)

    keys = jnp.concatenate([buf[me, 0, 0:KR, :], buf[me, 1, 0:KR, :]], axis=0)
    values = values_of(me)

    def own_scores(g):
        return jnp.dot(keys, qt[0:HD, g * C:(g + 1) * C], preferred_element_type=jnp.float32)

    ahead = own_scores(0)
    for g in range(G):
        score = ahead + bias[...]
        if g + 1 < G:
            ahead = own_scores(g + 1)
        high = jnp.max(score, axis=0, keepdims=True)
        weight = jnp.exp2(((score - high) * scale).astype(jnp.bfloat16))
        mx[g] = high
        acc[g] = jnp.dot(values, weight, preferred_element_type=jnp.float32)

    def step(s, unused):
        pass_up(s + 1)

        def entry(j):
            dx = lax.rem(j, X)
            p = jnp.where(j == X, s, s - 1)
            diagonal = j > X
            yy = jnp.where(diagonal | (j == 0), 1 - y, y)
            b = number(z - p, yy, xprev(dx))
            here = (p <= z) & need(b, z, y, x)

            @pl.when(here & diagonal)
            def _():
                copy(onward_x(dx), p, b, 0, side).wait_recv()
                copy(onward_y(dx), p, b, 1, side).wait_recv()

            @pl.when(here & (j == 0))
            def _():
                copy(3, p, b, 1, side).wait_recv()

            @pl.when(here & (j > 0) & (j < X))
            def _():
                copy(along_x(dx, 0), p, b, 0, side).wait_recv()

            return b, here

        def blocks(j, unused):
            @pl.when(j == X // 2)
            def _():
                pass_on(s)

            b0, shown0 = entry(2 * j)
            b1, shown1 = entry(2 * j + 1)

            @pl.when(shown0 & shown1)
            def _():
                attend(b0, b1)

            @pl.when(shown0 != shown1)
            def _():
                attend(jnp.where(shown0, b0, b1))

            return unused

        lax.fori_loop(0, X, blocks, 0)
        return unused

    lax.fori_loop(1, Z + 1, step, 0)

    mine = pl.ds(pl.multiple_of(c * T, T), T)
    theirs = pl.ds(pl.multiple_of(o * T, T), T)
    swaps = []
    for g in range(G):
        place = out_ref.at[:, pl.ds(pl.multiple_of(c * W + g * HD, HD), HD)]
        ostage[g] = (acc[g, 0:HD, theirs] / acc[g, HD:HD + 1, theirs]).astype(jnp.bfloat16).T
        swap = remote(ostage.at[g], place, out_send.at[g], out_recv.at[g], sibling)
        swap.start()
        swaps.append(swap)
        place[...] = (acc[g, 0:HD, mine] / acc[g, HD:HD + 1, mine]).astype(jnp.bfloat16).T

    def drain(s, unused):
        @pl.when(s <= z)
        def _():
            b = number(z - s, y, x)

            for half in range(2):
                @pl.when((z < Z - 1) & for_plane(b, z + 1))
                def _():
                    copy(half, s, b, half, up, s + 1).wait_send()

                @pl.when(for_row(b, 1 - y, half))
                def _():
                    copy(2 + half, s, b, half, side).wait_send()

                for dx in range(1, X):
                    @pl.when(for_column(b, xnext(dx), half))
                    def _():
                        copy(along_x(dx, half), s, b, half, side).wait_send()

            for dx in range(1, X):
                d = number(z - s, 1 - y, x)
                e = number(z - s, y, xprev(dx))

                @pl.when(need(d, z, y, xnext(dx)))
                def _():
                    copy(onward_x(dx), s, d, 0, side).wait_send()

                @pl.when(need(e, z, 1 - y, x))
                def _():
                    copy(onward_y(dx), s, e, 1, side).wait_send()

        return unused

    kv_swap.wait_send()
    q_swap.wait_send()
    lax.fori_loop(0, Z, drain, 0)
    for g in range(G):
        swaps[g].wait_send()
        place = out_ref.at[:, pl.ds(pl.multiple_of(o * W + g * HD, HD), HD)]
        remote(ostage.at[g], place, out_send.at[g], out_recv.at[g], sibling).wait_recv()


def shards(queries, keys_values, segment_ids, n_row, n_col):
    T = queries.shape[0]
    G = queries.shape[1] // (KVH * HD)
    Y = 2
    Z = n_row // Y
    X = n_col // 2
    chips = Z * Y * X
    kinds = 4 + 4 * (X - 1)
    C = 2 * T
    vmem = pl.BlockSpec(memory_space=pltpu.VMEM)
    dma = pltpu.SemaphoreType.DMA
    return pl.pallas_call(
        functools.partial(kernel, Z, Y, X, T, G),
        out_shape=jax.ShapeDtypeStruct(queries.shape, jnp.bfloat16),
        in_specs=[pl.BlockSpec(memory_space=pl.ANY), vmem, vmem],
        out_specs=vmem,
        scratch_shapes=[
            pltpu.VMEM((T, G * HD), jnp.bfloat16),
            dma,
            pltpu.VMEM((chips, 2, 2 * T + 16, HD), jnp.bfloat16),
            pltpu.VMEM((2 * T + 16, HD), jnp.bfloat16),
            pltpu.VMEM((T, G * HD), jnp.bfloat16),
            pltpu.VMEM((2 * HD, G * C), jnp.bfloat16),
            pltpu.VMEM((C, C), jnp.float32),
            pltpu.VMEM((G, 1, C), jnp.float32),
            pltpu.VMEM((G, HD + 16, C), jnp.float32),
            pltpu.VMEM((G, T, HD), jnp.bfloat16),
            dma((2,)),
            dma((2,)),
            dma((Z, kinds)),
            dma((Z, kinds)),
            dma((G,)),
            dma((G,)),
        ],
        compiler_params=pltpu.CompilerParams(
            collective_id=0, has_side_effects=True, vmem_limit_bytes=53 * 1024 * 1024
        ),
    )(queries, keys_values, segment_ids.reshape(1, T))


def solution(mesh):
    in_specs = (P(("row", "col"), None), P(("row", "col"), None), P(("row", "col")))
    out_specs = P(("row", "col"), None)
    body = functools.partial(shards, n_row=mesh.shape["row"], n_col=mesh.shape["col"])
    return jax.shard_map(body, mesh=mesh, in_specs=in_specs, out_specs=out_specs, check_vma=False)
```

```python
import functools
import math

import jax
import jax.numpy as jnp
from jax import lax
from jax.experimental import pallas as pl
from jax.experimental.pallas import tpu as pltpu
from jax.sharding import PartitionSpec as P

HD = 128
KVH = 2
BIG = 2.0**100
MESH = pl.DeviceIdType.MESH


def kernel(Z, Y, X, T, G, q_hbm, kv_hbm, seg_hbm, out_ref, q_ref, kv_ref, seg_ref, load, buf, stage, qrecv, qt, bias, mx, acc, ostage,
           pre_send, pre_recv, send, recv, out_send, out_recv):
    KR = T
    SR = T + 16
    row = lax.axis_index("row")
    col = lax.axis_index("col")
    z, y = row // Y, row % Y
    x, c = col // 2, col % 2
    o = 1 - c
    me = row * X + x
    C = 2 * T
    W = G * HD
    NX = X - 1
    reach = 3 * (Z * Y * X) // 4
    scale = math.log2(math.e) / math.sqrt(HD)

    def at(zz, yy, xx):
        return (zz * Y + yy, xx * 2 + c)

    sibling = (row, x * 2 + o)
    up = at(z + 1, y, x)
    side = at(z, 1 - y, x)

    def xnext(dx):
        return lax.rem(x + dx, X)

    def xprev(dx):
        return lax.rem(x - dx + X, X)

    q_load = pltpu.make_async_copy(q_hbm.at[:, pl.ds(pl.multiple_of(c * W, HD), W)], q_ref, load.at[0])
    kv_load = pltpu.make_async_copy(kv_hbm, kv_ref, load.at[1])
    seg_load = pltpu.make_async_copy(seg_hbm, seg_ref, load.at[2])
    kv_load.start()
    seg_load.start()
    q_load.start()

    barrier = pltpu.get_barrier_semaphore()
    pl.semaphore_signal(barrier, inc=1, device_id=sibling, device_id_type=MESH)
    pl.semaphore_signal(barrier, inc=1, device_id=side, device_id_type=MESH)
    for dx in range(1, X):
        pl.semaphore_signal(barrier, inc=1, device_id=at(z, y, xnext(dx)), device_id_type=MESH)

    @pl.when(z < Z - 1)
    def _():
        pl.semaphore_signal(barrier, inc=1, device_id=up, device_id_type=MESH)

    @pl.when(z > 0)
    def _():
        pl.semaphore_signal(barrier, inc=1, device_id=at(z - 1, y, x), device_id_type=MESH)

    kv_load.wait()
    seg_load.wait()

    seg16 = jnp.broadcast_to(seg_ref[...].astype(jnp.float32), (16, T)).astype(jnp.bfloat16)

    def piece(ref, h):
        ref[0:KR, :] = kv_ref[:, pl.ds(pl.multiple_of(h * HD, HD), HD)]
        ref[KR:SR, :] = seg16
        ref[SR:, :] = kv_ref[:, pl.ds(pl.multiple_of((KVH + h) * HD, HD), HD)].T

    piece(stage, o)
    pl.semaphore_wait(
        barrier, 2 + NX + jnp.where(z < Z - 1, 1, 0) + jnp.where(z > 0, 1, 0)
    )

    def remote(src, dst, s_sem, r_sem, device):
        return pltpu.make_async_remote_copy(
            src_ref=src, dst_ref=dst, send_sem=s_sem, recv_sem=r_sem, device_id=device, device_id_type=MESH
        )

    kv_swap = remote(stage, buf.at[me, c], pre_send.at[0], pre_recv.at[0], sibling)
    kv_swap.start()
    q_swap = remote(
        q_hbm.at[:, pl.ds(pl.multiple_of(o * W, HD), W)], qrecv, pre_send.at[1], pre_recv.at[1], sibling
    )
    q_swap.start()
    piece(buf.at[me, c], c)

    def number(zz, yy, xx):
        return (zz * Y + yy) * X + xx

    def along_x(dx, half):
        return 2 + 2 * dx + half

    def onward_x(dx):
        return 3 + 2 * NX + dx

    def onward_y(dx):
        return 3 + 3 * NX + dx

    def copy(kind, s, block, half, device, r_step=None):
        ref = buf.at[block, half]
        return remote(ref, ref, send.at[s, kind], recv.at[s if r_step is None else r_step, kind], device)

    def need(b, zz, yy, xx):
        i = number(zz, yy, xx)
        return (b < i) & (b >= i - reach)

    def for_row(b, yy, half):
        start = number(z, yy, 0)
        return jnp.where(half == 0, (b < start + X - 1) & (b >= start - reach), need(b, z, yy, x))

    def for_column(b, xx, half):
        return need(b, z, y, xx) | (need(b, z, 1 - y, xx) & (half == 1))

    def for_plane(b, zz):
        return b >= zz * Y * X - reach

    def send_half(s, half):
        b = number(z - s, y, x)

        @pl.when((s > 0) & for_plane(b, z))
        def _():
            copy(half, s, b, half, up).wait_recv()

        @pl.when((z < Z - 1) & for_plane(b, z + 1))
        def _():
            copy(half, s, b, half, up, s + 1).start()

        @pl.when(for_row(b, 1 - y, half))
        def _():
            copy(2 + half, s, b, half, side).start()

        for dx in range(1, X):
            @pl.when(for_column(b, xnext(dx), half))
            def _():
                copy(along_x(dx, half), s, b, half, at(z, y, xnext(dx))).start()

    def send_diagonal(s):
        b = number(z - s, 1 - y, x)

        @pl.when(for_row(b, y, 0))
        def _():
            copy(2, s, b, 0, side).wait_recv()

        for dx in range(1, X):
            @pl.when(need(b, z, y, xnext(dx)))
            def _():
                copy(onward_x(dx), s, b, 0, at(z, y, xnext(dx))).start()

        for dx in range(1, X):
            e = number(z - s, y, xprev(dx))

            @pl.when(for_column(e, x, 1))
            def _():
                copy(along_x(dx, 1), s, e, 1, side).wait_recv()

            @pl.when(need(e, z, 1 - y, x))
            def _():
                copy(onward_y(dx), s, e, 1, side).start()

    def pass_up(s):
        @pl.when(s <= z)
        def _():
            send_half(s, 0)
            send_half(s, 1)

    def pass_on(s):
        @pl.when(s <= z)
        def _():
            send_diagonal(s)

    start = jnp.int32(0)
    send_half(start, c)
    q_load.wait()
    for g in range(G):
        qt[0:HD, pl.ds(pl.multiple_of(g * C + c * T, T), T)] = q_ref[:, g * HD:(g + 1) * HD].T
    remote(stage, buf.at[me, o], pre_send.at[0], pre_recv.at[0], sibling).wait_recv()
    send_half(start, o)

    q_swap.wait_recv()
    for g in range(G):
        qt[0:HD, pl.ds(pl.multiple_of(g * C + o * T, T), T)] = qrecv[:, g * HD:(g + 1) * HD].T
    seg0 = buf[me, 0, KR:SR, :].astype(jnp.float32)
    seg1 = buf[me, 1, KR:SR, :].astype(jnp.float32)
    first = jnp.min(seg0, axis=1, keepdims=True)
    seg_q = jnp.concatenate([seg0, seg1], axis=1)
    hidden = jnp.where(seg_q == first, 0.0, -BIG)
    rows = lax.broadcasted_iota(jnp.int32, (16, C), 0)
    top16 = jnp.where(rows == 0, -BIG, jnp.where(rows == 1, hidden, 0.0)).astype(jnp.bfloat16)
    for g in range(G):
        qt[HD:HD + 16, g * C:(g + 1) * C] = top16
        qt[HD + 16:, g * C:(g + 1) * C] = jnp.zeros((HD - 16, C), jnp.bfloat16)
    turned = [jnp.broadcast_to(s[0:1, :], (T, T)).T for s in (seg0, seg1)]
    seg_k = jnp.concatenate(turned, axis=0)
    seg_k = jnp.concatenate([seg_k, seg_k], axis=1)
    k_at = lax.broadcasted_iota(jnp.int32, (C, C), 0)
    q_at = lax.broadcasted_iota(jnp.int32, (C, C), 1)
    bias[...] = jnp.where((seg_k == seg_q[0:1, :]) & (k_at <= q_at), 0.0, -BIG)

    lane = lax.broadcasted_iota(jnp.int32, (T, HD), 1)
    depth = lax.broadcasted_iota(jnp.int32, (T, HD), 0).astype(jnp.float32)

    def half_keys(b, half):
        seg = buf[b, half, KR:SR, :].astype(jnp.float32)
        shown = jnp.sum(jnp.where(seg == first, 1.0, 0.0), axis=1, keepdims=True)
        masked = jnp.where(depth < T - shown[0:1, :], 1.0, 0.0)
        extra = jnp.where(lane == 0, masked, 1.0).astype(jnp.bfloat16)
        return jnp.concatenate([buf[b, half, 0:KR, :], extra], axis=1)

    ones = jnp.ones((16, C), jnp.bfloat16)

    def values_of(b):
        values = jnp.concatenate([buf[b, 0, SR:, :], buf[b, 1, SR:, :]], axis=1)
        return jnp.concatenate([values, ones], axis=0)

    def keys_of(b):
        return jnp.concatenate([half_keys(b, 0), half_keys(b, 1)], axis=0)

    def attend(*blocks):
        keys = jnp.concatenate([keys_of(b) for b in blocks], axis=0)
        values = jnp.concatenate([values_of(b) for b in blocks], axis=1)

        def scores(g):
            return jnp.dot(keys, qt[:, g * C:(g + 1) * C], preferred_element_type=jnp.float32)

        def finish(g, factor, weight):
            acc[g] = acc[g] * factor + jnp.dot(values, weight, preferred_element_type=jnp.float32)

        ahead = scores(0)
        behind = None
        for g in range(G):
            score = ahead
            if g + 1 < G:
                ahead = scores(g + 1)
            old = mx[g]
            high = jnp.maximum(old, jnp.max(score, axis=0, keepdims=True))
            weight = jnp.exp2(((score - high) * scale).astype(jnp.bfloat16))
            factor = jnp.exp2((old - high) * scale)
            mx[g] = high
            if behind is not None:
                finish(*behind)
            behind = (g, factor, weight)
        finish(*behind)

    pass_up(jnp.int32(1))
    pass_on(start)

    keys = jnp.concatenate([buf[me, 0, 0:KR, :], buf[me, 1, 0:KR, :]], axis=0)
    values = values_of(me)

    def own_scores(g):
        return jnp.dot(keys, qt[0:HD, g * C:(g + 1) * C], preferred_element_type=jnp.float32)

    ahead = own_scores(0)
    for g in range(G):
        score = ahead + bias[...]
        if g + 1 < G:
            ahead = own_scores(g + 1)
        high = jnp.max(score, axis=0, keepdims=True)
        weight = jnp.exp2(((score - high) * scale).astype(jnp.bfloat16))
        mx[g] = high
        acc[g] = jnp.dot(values, weight, preferred_element_type=jnp.float32)

    def step(s, unused):
        pass_up(s + 1)

        def entry(j):
            dx = lax.rem(j, X)
            p = jnp.where(j == X, s, s - 1)
            diagonal = j > X
            yy = jnp.where(diagonal | (j == 0), 1 - y, y)
            b = number(z - p, yy, xprev(dx))
            here = (p <= z) & need(b, z, y, x)

            @pl.when(here & diagonal)
            def _():
                copy(onward_x(dx), p, b, 0, side).wait_recv()
                copy(onward_y(dx), p, b, 1, side).wait_recv()

            @pl.when(here & (j == 0))
            def _():
                copy(3, p, b, 1, side).wait_recv()

            @pl.when(here & (j > 0) & (j < X))
            def _():
                copy(along_x(dx, 0), p, b, 0, side).wait_recv()

            return b, here

        def blocks(j, unused):
            @pl.when((j == X // 2) & (s < z))
            def _():
                pass_on(s)

            b0, shown0 = entry(2 * j)
            b1, shown1 = entry(2 * j + 1)

            @pl.when(shown0 & shown1)
            def _():
                attend(b0, b1)

            @pl.when(shown0 != shown1)
            def _():
                attend(jnp.where(shown0, b0, b1))

            return unused

        lax.fori_loop(0, X, blocks, 0)

        @pl.when(s == z)
        def _():
            pass_on(s)

        return unused

    lax.fori_loop(1, Z + 1, step, 0)

    mine = pl.ds(pl.multiple_of(c * T, T), T)
    theirs = pl.ds(pl.multiple_of(o * T, T), T)
    swaps = []
    for g in range(G):
        place = out_ref.at[:, pl.ds(pl.multiple_of(c * W + g * HD, HD), HD)]
        ostage[g] = (acc[g, 0:HD, theirs] / acc[g, HD:HD + 1, theirs]).astype(jnp.bfloat16).T
        swap = remote(ostage.at[g], place, out_send.at[g], out_recv.at[g], sibling)
        swap.start()
        swaps.append(swap)
        place[...] = (acc[g, 0:HD, mine] / acc[g, HD:HD + 1, mine]).astype(jnp.bfloat16).T

    def drain(s, unused):
        @pl.when(s <= z)
        def _():
            b = number(z - s, y, x)

            for half in range(2):
                @pl.when((z < Z - 1) & for_plane(b, z + 1))
                def _():
                    copy(half, s, b, half, up, s + 1).wait_send()

                @pl.when(for_row(b, 1 - y, half))
                def _():
                    copy(2 + half, s, b, half, side).wait_send()

                for dx in range(1, X):
                    @pl.when(for_column(b, xnext(dx), half))
                    def _():
                        copy(along_x(dx, half), s, b, half, side).wait_send()

            for dx in range(1, X):
                d = number(z - s, 1 - y, x)
                e = number(z - s, y, xprev(dx))

                @pl.when(need(d, z, y, xnext(dx)))
                def _():
                    copy(onward_x(dx), s, d, 0, side).wait_send()

                @pl.when(need(e, z, 1 - y, x))
                def _():
                    copy(onward_y(dx), s, e, 1, side).wait_send()

        return unused

    kv_swap.wait_send()
    q_swap.wait_send()
    lax.fori_loop(0, Z, drain, 0)
    for g in range(G):
        swaps[g].wait_send()
        place = out_ref.at[:, pl.ds(pl.multiple_of(o * W + g * HD, HD), HD)]
        remote(ostage.at[g], place, out_send.at[g], out_recv.at[g], sibling).wait_recv()


def shards(queries, keys_values, segment_ids, n_row, n_col):
    T = queries.shape[0]
    G = queries.shape[1] // (KVH * HD)
    Y = 2
    Z = n_row // Y
    X = n_col // 2
    chips = Z * Y * X
    kinds = 4 + 4 * (X - 1)
    C = 2 * T
    vmem = pl.BlockSpec(memory_space=pltpu.VMEM)
    dma = pltpu.SemaphoreType.DMA
    return pl.pallas_call(
        functools.partial(kernel, Z, Y, X, T, G),
        out_shape=pltpu.VMEM(queries.shape, jnp.bfloat16),
        in_specs=[pl.BlockSpec(memory_space=pl.ANY)] * 3,
        out_specs=vmem,
        scratch_shapes=[
            pltpu.VMEM((T, G * HD), jnp.bfloat16),
            pltpu.VMEM(keys_values.shape, jnp.bfloat16),
            pltpu.VMEM((1, T), jnp.int32),
            dma((3,)),
            pltpu.VMEM((chips, 2, 2 * T + 16, HD), jnp.bfloat16),
            pltpu.VMEM((2 * T + 16, HD), jnp.bfloat16),
            pltpu.VMEM((T, G * HD), jnp.bfloat16),
            pltpu.VMEM((2 * HD, G * C), jnp.bfloat16),
            pltpu.VMEM((C, C), jnp.float32),
            pltpu.VMEM((G, 1, C), jnp.float32),
            pltpu.VMEM((G, HD + 16, C), jnp.float32),
            pltpu.VMEM((G, T, HD), jnp.bfloat16),
            dma((2,)),
            dma((2,)),
            dma((Z, kinds)),
            dma((Z, kinds)),
            dma((G,)),
            dma((G,)),
        ],
        compiler_params=pltpu.CompilerParams(
            collective_id=0, has_side_effects=True, vmem_limit_bytes=60 * 1024 * 1024
        ),
    )(queries, keys_values, segment_ids.reshape(1, T))


def solution(mesh):
    in_specs = (P(("row", "col"), None), P(("row", "col"), None), P(("row", "col")))
    out_specs = P(("row", "col"), None)
    body = functools.partial(shards, n_row=mesh.shape["row"], n_col=mesh.shape["col"])
    return jax.shard_map(body, mesh=mesh, in_specs=in_specs, out_specs=out_specs, check_vma=False)
```

```python
import functools
import math

import jax
import jax.numpy as jnp
from jax import lax
from jax.experimental import pallas as pl
from jax.experimental.pallas import tpu as pltpu
from jax.sharding import PartitionSpec as P

HD = 128
KVH = 2
BIG = 2.0**100
MESH = pl.DeviceIdType.MESH


def kernel(Z, Y, X, T, G, q_hbm, kv_ref, seg_ref, out_ref, q_ref, load, buf, stage, qrecv, qt, bias, mx, acc, ostage,
           pre_send, pre_recv, send, recv, out_send, out_recv):
    KR = T
    SR = T + 16
    row = lax.axis_index("row")
    col = lax.axis_index("col")
    z, y = row // Y, row % Y
    x, c = col // 2, col % 2
    o = 1 - c
    me = row * X + x
    C = 2 * T
    W = G * HD
    NX = X - 1
    reach = 3 * (Z * Y * X) // 4
    scale = math.log2(math.e) / math.sqrt(HD)

    def at(zz, yy, xx):
        return (zz * Y + yy, xx * 2 + c)

    sibling = (row, x * 2 + o)
    up = at(z + 1, y, x)
    side = at(z, 1 - y, x)

    def xnext(dx):
        return lax.rem(x + dx, X)

    def xprev(dx):
        return lax.rem(x - dx + X, X)

    q_load = pltpu.make_async_copy(q_hbm.at[:, pl.ds(pl.multiple_of(c * W, HD), W)], q_ref, load)
    q_load.start()

    barrier = pltpu.get_barrier_semaphore()
    pl.semaphore_signal(barrier, inc=1, device_id=sibling, device_id_type=MESH)
    pl.semaphore_signal(barrier, inc=1, device_id=side, device_id_type=MESH)
    for dx in range(1, X):
        pl.semaphore_signal(barrier, inc=1, device_id=at(z, y, xnext(dx)), device_id_type=MESH)

    @pl.when(z < Z - 1)
    def _():
        pl.semaphore_signal(barrier, inc=1, device_id=up, device_id_type=MESH)

    @pl.when(z > 0)
    def _():
        pl.semaphore_signal(barrier, inc=1, device_id=at(z - 1, y, x), device_id_type=MESH)

    seg16 = jnp.broadcast_to(seg_ref[...].astype(jnp.float32), (16, T)).astype(jnp.bfloat16)

    def piece(ref, h):
        ref[0:KR, :] = kv_ref[:, pl.ds(pl.multiple_of(h * HD, HD), HD)]
        ref[KR:SR, :] = seg16
        ref[SR:, :] = kv_ref[:, pl.ds(pl.multiple_of((KVH + h) * HD, HD), HD)].T

    piece(stage, o)
    pl.semaphore_wait(
        barrier, 2 + NX + jnp.where(z < Z - 1, 1, 0) + jnp.where(z > 0, 1, 0)
    )

    def remote(src, dst, s_sem, r_sem, device):
        return pltpu.make_async_remote_copy(
            src_ref=src, dst_ref=dst, send_sem=s_sem, recv_sem=r_sem, device_id=device, device_id_type=MESH
        )

    kv_swap = remote(stage, buf.at[me, c], pre_send.at[0], pre_recv.at[0], sibling)
    kv_swap.start()
    q_swap = remote(
        q_hbm.at[:, pl.ds(pl.multiple_of(o * W, HD), W)], qrecv, pre_send.at[1], pre_recv.at[1], sibling
    )
    q_swap.start()
    piece(buf.at[me, c], c)

    def number(zz, yy, xx):
        return (zz * Y + yy) * X + xx

    def along_x(dx, half):
        return 2 + 2 * dx + half

    def onward_x(dx):
        return 3 + 2 * NX + dx

    def onward_y(dx):
        return 3 + 3 * NX + dx

    def copy(kind, s, block, half, device, r_step=None):
        ref = buf.at[block, half]
        return remote(ref, ref, send.at[s, kind], recv.at[s if r_step is None else r_step, kind], device)

    def need(b, zz, yy, xx):
        i = number(zz, yy, xx)
        return (b < i) & (b >= i - reach)

    def for_row(b, yy, half):
        start = number(z, yy, 0)
        return jnp.where(half == 0, (b < start + X - 1) & (b >= start - reach), need(b, z, yy, x))

    def for_column(b, xx, half):
        return need(b, z, y, xx) | (need(b, z, 1 - y, xx) & (half == 1))

    def for_plane(b, zz):
        return b >= zz * Y * X - reach

    def lift(s, half):
        b = number(z - s, y, x)

        @pl.when((s > 0) & for_plane(b, z))
        def _():
            copy(half, s, b, half, up).wait_recv()

        @pl.when((z < Z - 1) & for_plane(b, z + 1))
        def _():
            copy(half, s, b, half, up, s + 1).start()

    def send_y(s, half):
        b = number(z - s, y, x)

        @pl.when(for_row(b, 1 - y, half))
        def _():
            copy(2 + half, s, b, half, side).start()

    def send_x(s, half):
        b = number(z - s, y, x)

        for dx in range(1, X):
            @pl.when(for_column(b, xnext(dx), half))
            def _():
                copy(along_x(dx, half), s, b, half, at(z, y, xnext(dx))).start()

    def send_diagonal(s):
        b = number(z - s, 1 - y, x)

        @pl.when(for_row(b, y, 0))
        def _():
            copy(2, s, b, 0, side).wait_recv()

        for dx in range(1, X):
            @pl.when(need(b, z, y, xnext(dx)))
            def _():
                copy(onward_x(dx), s, b, 0, at(z, y, xnext(dx))).start()

        for dx in range(1, X):
            e = number(z - s, y, xprev(dx))

            @pl.when(for_column(e, x, 1))
            def _():
                copy(along_x(dx, 1), s, e, 1, side).wait_recv()

            @pl.when(need(e, z, 1 - y, x))
            def _():
                copy(onward_y(dx), s, e, 1, side).start()

    def send_half(s, half):
        lift(s, half)
        send_y(s, half)
        send_x(s, half)

    def pass_up(s):
        @pl.when(s <= z)
        def _():
            lift(s, 0)
            send_y(s, 0)
            lift(s, 1)
            send_x(s, 1)
            send_y(s, 1)
            send_x(s, 0)

    def pass_on(s):
        @pl.when(s <= z)
        def _():
            send_diagonal(s)

    start = jnp.int32(0)
    send_half(start, c)
    q_load.wait()
    for g in range(G):
        qt[0:HD, pl.ds(pl.multiple_of(g * C + c * T, T), T)] = q_ref[:, g * HD:(g + 1) * HD].T
    remote(stage, buf.at[me, o], pre_send.at[0], pre_recv.at[0], sibling).wait_recv()
    send_half(start, o)

    q_swap.wait_recv()
    for g in range(G):
        qt[0:HD, pl.ds(pl.multiple_of(g * C + o * T, T), T)] = qrecv[:, g * HD:(g + 1) * HD].T
    seg0 = buf[me, 0, KR:SR, :].astype(jnp.float32)
    seg1 = buf[me, 1, KR:SR, :].astype(jnp.float32)
    first = jnp.min(seg0, axis=1, keepdims=True)
    seg_q = jnp.concatenate([seg0, seg1], axis=1)
    hidden = jnp.where(seg_q == first, 0.0, -BIG)
    rows = lax.broadcasted_iota(jnp.int32, (16, C), 0)
    top16 = jnp.where(rows == 0, -BIG, jnp.where(rows == 1, hidden, 0.0)).astype(jnp.bfloat16)
    for g in range(G):
        qt[HD:HD + 16, g * C:(g + 1) * C] = top16
        qt[HD + 16:, g * C:(g + 1) * C] = jnp.zeros((HD - 16, C), jnp.bfloat16)
    turned = [jnp.broadcast_to(s[0:1, :], (T, T)).T for s in (seg0, seg1)]
    seg_k = jnp.concatenate(turned, axis=0)
    seg_k = jnp.concatenate([seg_k, seg_k], axis=1)
    k_at = lax.broadcasted_iota(jnp.int32, (C, C), 0)
    q_at = lax.broadcasted_iota(jnp.int32, (C, C), 1)
    bias[...] = jnp.where((seg_k == seg_q[0:1, :]) & (k_at <= q_at), 0.0, -BIG)

    lane = lax.broadcasted_iota(jnp.int32, (T, HD), 1)
    depth = lax.broadcasted_iota(jnp.int32, (T, HD), 0).astype(jnp.float32)

    def half_keys(b, half):
        seg = buf[b, half, KR:SR, :].astype(jnp.float32)
        shown = jnp.sum(jnp.where(seg == first, 1.0, 0.0), axis=1, keepdims=True)
        masked = jnp.where(depth < T - shown[0:1, :], 1.0, 0.0)
        extra = jnp.where(lane == 0, masked, 1.0).astype(jnp.bfloat16)
        return jnp.concatenate([buf[b, half, 0:KR, :], extra], axis=1)

    ones = jnp.ones((16, C), jnp.bfloat16)

    def values_of(b):
        values = jnp.concatenate([buf[b, 0, SR:, :], buf[b, 1, SR:, :]], axis=1)
        return jnp.concatenate([values, ones], axis=0)

    def keys_of(b):
        return jnp.concatenate([half_keys(b, 0), half_keys(b, 1)], axis=0)

    def attend(*blocks):
        keys = jnp.concatenate([keys_of(b) for b in blocks], axis=0)
        values = jnp.concatenate([values_of(b) for b in blocks], axis=1)

        def scores(g):
            return jnp.dot(keys, qt[:, g * C:(g + 1) * C], preferred_element_type=jnp.float32)

        def finish(g, factor, weight):
            acc[g] = acc[g] * factor + jnp.dot(values, weight, preferred_element_type=jnp.float32)

        ahead = scores(0)
        behind = None
        for g in range(G):
            score = ahead
            if g + 1 < G:
                ahead = scores(g + 1)
            old = mx[g]
            high = jnp.maximum(old, jnp.max(score, axis=0, keepdims=True))
            weight = jnp.exp2(((score - high) * scale).astype(jnp.bfloat16))
            factor = jnp.exp2((old - high) * scale)
            mx[g] = high
            if behind is not None:
                finish(*behind)
            behind = (g, factor, weight)
        finish(*behind)

    pass_up(jnp.int32(1))
    pass_on(start)

    keys = jnp.concatenate([buf[me, 0, 0:KR, :], buf[me, 1, 0:KR, :]], axis=0)
    values = values_of(me)

    def own_scores(g):
        return jnp.dot(keys, qt[0:HD, g * C:(g + 1) * C], preferred_element_type=jnp.float32)

    ahead = own_scores(0)
    for g in range(G):
        score = ahead + bias[...]
        if g + 1 < G:
            ahead = own_scores(g + 1)
        high = jnp.max(score, axis=0, keepdims=True)
        weight = jnp.exp2(((score - high) * scale).astype(jnp.bfloat16))
        mx[g] = high
        acc[g] = jnp.dot(values, weight, preferred_element_type=jnp.float32)

    def step(s, unused):
        pass_up(s + 1)

        def entry(j):
            dx = lax.rem(j, X)
            p = jnp.where(j == X, s, s - 1)
            diagonal = j > X
            yy = jnp.where(diagonal | (j == 0), 1 - y, y)
            b = number(z - p, yy, xprev(dx))
            here = (p <= z) & need(b, z, y, x)

            @pl.when(here & diagonal)
            def _():
                copy(onward_x(dx), p, b, 0, side).wait_recv()
                copy(onward_y(dx), p, b, 1, side).wait_recv()

            @pl.when(here & (j == 0))
            def _():
                copy(3, p, b, 1, side).wait_recv()

            @pl.when(here & (j > 0) & (j < X))
            def _():
                copy(along_x(dx, 0), p, b, 0, side).wait_recv()

            return b, here

        def blocks(j, unused):
            @pl.when(j == X // 2)
            def _():
                pass_on(s)

            b0, shown0 = entry(2 * j)
            b1, shown1 = entry(2 * j + 1)

            @pl.when(shown0 & shown1)
            def _():
                attend(b0, b1)

            @pl.when(shown0 != shown1)
            def _():
                attend(jnp.where(shown0, b0, b1))

            return unused

        lax.fori_loop(0, X, blocks, 0)
        return unused

    lax.fori_loop(1, Z + 1, step, 0)

    mine = pl.ds(pl.multiple_of(c * T, T), T)
    theirs = pl.ds(pl.multiple_of(o * T, T), T)
    swaps = []
    for g in range(G):
        place = out_ref.at[:, pl.ds(pl.multiple_of(c * W + g * HD, HD), HD)]
        ostage[g] = (acc[g, 0:HD, theirs] / acc[g, HD:HD + 1, theirs]).astype(jnp.bfloat16).T
        swap = remote(ostage.at[g], place, out_send.at[g], out_recv.at[g], sibling)
        swap.start()
        swaps.append(swap)
        place[...] = (acc[g, 0:HD, mine] / acc[g, HD:HD + 1, mine]).astype(jnp.bfloat16).T

    def drain(s, unused):
        @pl.when(s <= z)
        def _():
            b = number(z - s, y, x)

            for half in range(2):
                @pl.when((z < Z - 1) & for_plane(b, z + 1))
                def _():
                    copy(half, s, b, half, up, s + 1).wait_send()

                @pl.when(for_row(b, 1 - y, half))
                def _():
                    copy(2 + half, s, b, half, side).wait_send()

                for dx in range(1, X):
                    @pl.when(for_column(b, xnext(dx), half))
                    def _():
                        copy(along_x(dx, half), s, b, half, side).wait_send()

            for dx in range(1, X):
                d = number(z - s, 1 - y, x)
                e = number(z - s, y, xprev(dx))

                @pl.when(need(d, z, y, xnext(dx)))
                def _():
                    copy(onward_x(dx), s, d, 0, side).wait_send()

                @pl.when(need(e, z, 1 - y, x))
                def _():
                    copy(onward_y(dx), s, e, 1, side).wait_send()

        return unused

    kv_swap.wait_send()
    q_swap.wait_send()
    lax.fori_loop(0, Z, drain, 0)
    for g in range(G):
        swaps[g].wait_send()
        place = out_ref.at[:, pl.ds(pl.multiple_of(o * W + g * HD, HD), HD)]
        remote(ostage.at[g], place, out_send.at[g], out_recv.at[g], sibling).wait_recv()


def shards(queries, keys_values, segment_ids, n_row, n_col):
    T = queries.shape[0]
    G = queries.shape[1] // (KVH * HD)
    Y = 2
    Z = n_row // Y
    X = n_col // 2
    chips = Z * Y * X
    kinds = 4 + 4 * (X - 1)
    C = 2 * T
    vmem = pl.BlockSpec(memory_space=pltpu.VMEM)
    dma = pltpu.SemaphoreType.DMA
    return pl.pallas_call(
        functools.partial(kernel, Z, Y, X, T, G),
        out_shape=jax.ShapeDtypeStruct(queries.shape, jnp.bfloat16),
        in_specs=[pl.BlockSpec(memory_space=pl.ANY), vmem, vmem],
        out_specs=vmem,
        scratch_shapes=[
            pltpu.VMEM((T, G * HD), jnp.bfloat16),
            dma,
            pltpu.VMEM((chips, 2, 2 * T + 16, HD), jnp.bfloat16),
            pltpu.VMEM((2 * T + 16, HD), jnp.bfloat16),
            pltpu.VMEM((T, G * HD), jnp.bfloat16),
            pltpu.VMEM((2 * HD, G * C), jnp.bfloat16),
            pltpu.VMEM((C, C), jnp.float32),
            pltpu.VMEM((G, 1, C), jnp.float32),
            pltpu.VMEM((G, HD + 16, C), jnp.float32),
            pltpu.VMEM((G, T, HD), jnp.bfloat16),
            dma((2,)),
            dma((2,)),
            dma((Z, kinds)),
            dma((Z, kinds)),
            dma((G,)),
            dma((G,)),
        ],
        compiler_params=pltpu.CompilerParams(
            collective_id=0, has_side_effects=True, vmem_limit_bytes=53 * 1024 * 1024
        ),
    )(queries, keys_values, segment_ids.reshape(1, T))


def solution(mesh):
    in_specs = (P(("row", "col"), None), P(("row", "col"), None), P(("row", "col")))
    out_specs = P(("row", "col"), None)
    body = functools.partial(shards, n_row=mesh.shape["row"], n_col=mesh.shape["col"])
    return jax.shard_map(body, mesh=mesh, in_specs=in_specs, out_specs=out_specs, check_vma=False)
```

```python
import functools
import math

import jax
import jax.numpy as jnp
from jax import lax
from jax.experimental import pallas as pl
from jax.experimental.pallas import tpu as pltpu
from jax.sharding import PartitionSpec as P

HD = 128
KVH = 2
BIG = 2.0**100
MESH = pl.DeviceIdType.MESH


def kernel(Z, Y, X, T, G, q_hbm, kv_ref, seg_ref, out_ref, q_ref, load, buf, stage, qrecv, qt, bias, mx, acc, ostage,
           pre_send, pre_recv, send, recv, out_send, out_recv):
    KR = T
    SR = T + 16
    row = lax.axis_index("row")
    col = lax.axis_index("col")
    z, y = row // Y, row % Y
    x, c = col // 2, col % 2
    o = 1 - c
    me = row * X + x
    C = 2 * T
    W = G * HD
    NX = X - 1
    reach = 3 * (Z * Y * X) // 4
    scale = math.log2(math.e) / math.sqrt(HD)

    def at(zz, yy, xx):
        return (zz * Y + yy, xx * 2 + c)

    sibling = (row, x * 2 + o)
    up = at(z + 1, y, x)
    side = at(z, 1 - y, x)

    def xnext(dx):
        return lax.rem(x + dx, X)

    def xprev(dx):
        return lax.rem(x - dx + X, X)

    q_load = pltpu.make_async_copy(q_hbm.at[:, pl.ds(pl.multiple_of(c * W, HD), W)], q_ref, load)
    q_load.start()

    barrier = pltpu.get_barrier_semaphore()
    pl.semaphore_signal(barrier, inc=1, device_id=sibling, device_id_type=MESH)
    pl.semaphore_signal(barrier, inc=1, device_id=side, device_id_type=MESH)
    for dx in range(1, X):
        pl.semaphore_signal(barrier, inc=1, device_id=at(z, y, xnext(dx)), device_id_type=MESH)

    @pl.when(z < Z - 1)
    def _():
        pl.semaphore_signal(barrier, inc=1, device_id=up, device_id_type=MESH)

    @pl.when(z > 0)
    def _():
        pl.semaphore_signal(barrier, inc=1, device_id=at(z - 1, y, x), device_id_type=MESH)

    seg16 = jnp.broadcast_to(seg_ref[...].astype(jnp.float32), (16, T)).astype(jnp.bfloat16)

    def piece(ref, h):
        ref[0:KR, :] = kv_ref[:, pl.ds(pl.multiple_of(h * HD, HD), HD)]
        ref[KR:SR, :] = seg16
        ref[SR:, :] = kv_ref[:, pl.ds(pl.multiple_of((KVH + h) * HD, HD), HD)].T

    piece(stage, o)
    piece(buf.at[me, c], c)
    for g in range(G):
        qt[HD + 16:, g * C:(g + 1) * C] = jnp.zeros((HD - 16, C), jnp.bfloat16)
    pl.semaphore_wait(
        barrier, 2 + NX + jnp.where(z < Z - 1, 1, 0) + jnp.where(z > 0, 1, 0)
    )

    def remote(src, dst, s_sem, r_sem, device):
        return pltpu.make_async_remote_copy(
            src_ref=src, dst_ref=dst, send_sem=s_sem, recv_sem=r_sem, device_id=device, device_id_type=MESH
        )

    kv_swap = remote(stage, buf.at[me, c], pre_send.at[0], pre_recv.at[0], sibling)
    kv_swap.start()
    q_swap = remote(
        q_hbm.at[:, pl.ds(pl.multiple_of(o * W, HD), W)], qrecv, pre_send.at[1], pre_recv.at[1], sibling
    )
    q_swap.start()

    def number(zz, yy, xx):
        return (zz * Y + yy) * X + xx

    def along_x(dx, half):
        return 2 + 2 * dx + half

    def onward_x(dx):
        return 3 + 2 * NX + dx

    def onward_y(dx):
        return 3 + 3 * NX + dx

    def copy(kind, s, block, half, device, r_step=None):
        ref = buf.at[block, half]
        return remote(ref, ref, send.at[s, kind], recv.at[s if r_step is None else r_step, kind], device)

    def need(b, zz, yy, xx):
        i = number(zz, yy, xx)
        return (b < i) & (b >= i - reach)

    def for_row(b, yy, half):
        start = number(z, yy, 0)
        return jnp.where(half == 0, (b < start + X - 1) & (b >= start - reach), need(b, z, yy, x))

    def for_column(b, xx, half):
        return need(b, z, y, xx) | (need(b, z, 1 - y, xx) & (half == 1))

    def for_plane(b, zz):
        return b >= zz * Y * X - reach

    def send_half(s, half):
        b = number(z - s, y, x)

        @pl.when((s > 0) & for_plane(b, z))
        def _():
            copy(half, s, b, half, up).wait_recv()

        @pl.when((z < Z - 1) & for_plane(b, z + 1))
        def _():
            copy(half, s, b, half, up, s + 1).start()

        @pl.when(for_row(b, 1 - y, half))
        def _():
            copy(2 + half, s, b, half, side).start()

        for dx in range(1, X):
            @pl.when(for_column(b, xnext(dx), half))
            def _():
                copy(along_x(dx, half), s, b, half, at(z, y, xnext(dx))).start()

    def send_diagonal(s):
        b = number(z - s, 1 - y, x)

        @pl.when(for_row(b, y, 0))
        def _():
            copy(2, s, b, 0, side).wait_recv()

        for dx in range(1, X):
            @pl.when(need(b, z, y, xnext(dx)))
            def _():
                copy(onward_x(dx), s, b, 0, at(z, y, xnext(dx))).start()

        for dx in range(1, X):
            e = number(z - s, y, xprev(dx))

            @pl.when(for_column(e, x, 1))
            def _():
                copy(along_x(dx, 1), s, e, 1, side).wait_recv()

            @pl.when(need(e, z, 1 - y, x))
            def _():
                copy(onward_y(dx), s, e, 1, side).start()

    def pass_up(s):
        @pl.when(s <= z)
        def _():
            send_half(s, 0)
            send_half(s, 1)

    def pass_on(s):
        @pl.when(s <= z)
        def _():
            send_diagonal(s)

    start = jnp.int32(0)
    send_half(start, c)
    q_load.wait()
    for g in range(G):
        qt[0:HD, pl.ds(pl.multiple_of(g * C + c * T, T), T)] = q_ref[:, g * HD:(g + 1) * HD].T
    remote(stage, buf.at[me, o], pre_send.at[0], pre_recv.at[0], sibling).wait_recv()
    send_half(start, o)

    q_swap.wait_recv()
    for g in range(G):
        qt[0:HD, pl.ds(pl.multiple_of(g * C + o * T, T), T)] = qrecv[:, g * HD:(g + 1) * HD].T
    seg0 = buf[me, 0, KR:SR, :].astype(jnp.float32)
    seg1 = buf[me, 1, KR:SR, :].astype(jnp.float32)
    first = jnp.min(seg0, axis=1, keepdims=True)
    seg_q = jnp.concatenate([seg0, seg1], axis=1)
    hidden = jnp.where(seg_q == first, 0.0, -BIG)
    rows = lax.broadcasted_iota(jnp.int32, (16, C), 0)
    top16 = jnp.where(rows == 0, -BIG, jnp.where(rows == 1, hidden, 0.0)).astype(jnp.bfloat16)
    for g in range(G):
        qt[HD:HD + 16, g * C:(g + 1) * C] = top16
    turned = [jnp.broadcast_to(s[0:1, :], (T, T)).T for s in (seg0, seg1)]
    seg_k = jnp.concatenate(turned, axis=0)
    seg_k = jnp.concatenate([seg_k, seg_k], axis=1)
    k_at = lax.broadcasted_iota(jnp.int32, (C, C), 0)
    q_at = lax.broadcasted_iota(jnp.int32, (C, C), 1)
    bias[...] = jnp.where((seg_k == seg_q[0:1, :]) & (k_at <= q_at), 0.0, -BIG)

    lane = lax.broadcasted_iota(jnp.int32, (T, HD), 1)
    depth = lax.broadcasted_iota(jnp.int32, (T, HD), 0).astype(jnp.float32)

    def half_keys(b, half):
        seg = buf[b, half, KR:SR, :].astype(jnp.float32)
        shown = jnp.sum(jnp.where(seg == first, 1.0, 0.0), axis=1, keepdims=True)
        masked = jnp.where(depth < T - shown[0:1, :], 1.0, 0.0)
        extra = jnp.where(lane == 0, masked, 1.0).astype(jnp.bfloat16)
        return jnp.concatenate([buf[b, half, 0:KR, :], extra], axis=1)

    ones = jnp.ones((16, C), jnp.bfloat16)

    def values_of(b):
        values = jnp.concatenate([buf[b, 0, SR:, :], buf[b, 1, SR:, :]], axis=1)
        return jnp.concatenate([values, ones], axis=0)

    def keys_of(b):
        return jnp.concatenate([half_keys(b, 0), half_keys(b, 1)], axis=0)

    def attend(*blocks):
        keys = jnp.concatenate([keys_of(b) for b in blocks], axis=0)
        values = jnp.concatenate([values_of(b) for b in blocks], axis=1)

        def scores(g):
            return jnp.dot(keys, qt[:, g * C:(g + 1) * C], preferred_element_type=jnp.float32)

        def finish(g, factor, weight):
            acc[g] = acc[g] * factor + jnp.dot(values, weight, preferred_element_type=jnp.float32)

        ahead = scores(0)
        behind = None
        for g in range(G):
            score = ahead
            if g + 1 < G:
                ahead = scores(g + 1)
            old = mx[g]
            high = jnp.maximum(old, jnp.max(score, axis=0, keepdims=True))
            weight = jnp.exp2(((score - high) * scale).astype(jnp.bfloat16))
            factor = jnp.exp2((old - high) * scale)
            mx[g] = high
            if behind is not None:
                finish(*behind)
            behind = (g, factor, weight)
        finish(*behind)

    pass_up(jnp.int32(1))
    pass_on(start)

    keys = jnp.concatenate([buf[me, 0, 0:KR, :], buf[me, 1, 0:KR, :]], axis=0)
    values = values_of(me)

    def own_scores(g):
        return jnp.dot(keys, qt[0:HD, g * C:(g + 1) * C], preferred_element_type=jnp.float32)

    ahead = own_scores(0)
    for g in range(G):
        score = ahead + bias[...]
        if g + 1 < G:
            ahead = own_scores(g + 1)
        high = jnp.max(score, axis=0, keepdims=True)
        weight = jnp.exp2(((score - high) * scale).astype(jnp.bfloat16))
        mx[g] = high
        acc[g] = jnp.dot(values, weight, preferred_element_type=jnp.float32)

    def step(s, unused):
        pass_up(s + 1)

        def entry(j):
            dx = lax.rem(j, X)
            p = jnp.where(j == X, s, s - 1)
            diagonal = j > X
            yy = jnp.where(diagonal | (j == 0), 1 - y, y)
            b = number(z - p, yy, xprev(dx))
            here = (p <= z) & need(b, z, y, x)

            @pl.when(here & diagonal)
            def _():
                copy(onward_x(dx), p, b, 0, side).wait_recv()
                copy(onward_y(dx), p, b, 1, side).wait_recv()

            @pl.when(here & (j == 0))
            def _():
                copy(3, p, b, 1, side).wait_recv()

            @pl.when(here & (j > 0) & (j < X))
            def _():
                copy(along_x(dx, 0), p, b, 0, side).wait_recv()

            return b, here

        def blocks(j, unused):
            @pl.when(j == X // 2)
            def _():
                pass_on(s)

            b0, shown0 = entry(2 * j)
            b1, shown1 = entry(2 * j + 1)

            @pl.when(shown0 & shown1)
            def _():
                attend(b0, b1)

            @pl.when(shown0 != shown1)
            def _():
                attend(jnp.where(shown0, b0, b1))

            return unused

        lax.fori_loop(0, X, blocks, 0)
        return unused

    lax.fori_loop(1, Z + 1, step, 0)

    mine = pl.ds(pl.multiple_of(c * T, T), T)
    theirs = pl.ds(pl.multiple_of(o * T, T), T)
    swaps = []
    for g in range(G):
        place = out_ref.at[:, pl.ds(pl.multiple_of(c * W + g * HD, HD), HD)]
        ostage[g] = (acc[g, 0:HD, theirs] * (1.0 / acc[g, HD:HD + 1, theirs])).astype(jnp.bfloat16).T
        swap = remote(ostage.at[g], place, out_send.at[g], out_recv.at[g], sibling)
        swap.start()
        swaps.append(swap)
    for g in range(G):
        place = out_ref.at[:, pl.ds(pl.multiple_of(c * W + g * HD, HD), HD)]
        place[...] = (acc[g, 0:HD, mine] * (1.0 / acc[g, HD:HD + 1, mine])).astype(jnp.bfloat16).T

    def drain(s, unused):
        @pl.when(s <= z)
        def _():
            b = number(z - s, y, x)

            for half in range(2):
                @pl.when((z < Z - 1) & for_plane(b, z + 1))
                def _():
                    copy(half, s, b, half, up, s + 1).wait_send()

                @pl.when(for_row(b, 1 - y, half))
                def _():
                    copy(2 + half, s, b, half, side).wait_send()

                for dx in range(1, X):
                    @pl.when(for_column(b, xnext(dx), half))
                    def _():
                        copy(along_x(dx, half), s, b, half, side).wait_send()

            for dx in range(1, X):
                d = number(z - s, 1 - y, x)
                e = number(z - s, y, xprev(dx))

                @pl.when(need(d, z, y, xnext(dx)))
                def _():
                    copy(onward_x(dx), s, d, 0, side).wait_send()

                @pl.when(need(e, z, 1 - y, x))
                def _():
                    copy(onward_y(dx), s, e, 1, side).wait_send()

        return unused

    kv_swap.wait_send()
    q_swap.wait_send()
    lax.fori_loop(0, Z, drain, 0)
    for g in range(G):
        swaps[g].wait_send()
        place = out_ref.at[:, pl.ds(pl.multiple_of(o * W + g * HD, HD), HD)]
        remote(ostage.at[g], place, out_send.at[g], out_recv.at[g], sibling).wait_recv()


def shards(queries, keys_values, segment_ids, n_row, n_col):
    T = queries.shape[0]
    G = queries.shape[1] // (KVH * HD)
    Y = 2
    Z = n_row // Y
    X = n_col // 2
    chips = Z * Y * X
    kinds = 4 + 4 * (X - 1)
    C = 2 * T
    vmem = pl.BlockSpec(memory_space=pltpu.VMEM)
    dma = pltpu.SemaphoreType.DMA
    return pl.pallas_call(
        functools.partial(kernel, Z, Y, X, T, G),
        out_shape=jax.ShapeDtypeStruct(queries.shape, jnp.bfloat16),
        in_specs=[pl.BlockSpec(memory_space=pl.ANY), vmem, vmem],
        out_specs=vmem,
        scratch_shapes=[
            pltpu.VMEM((T, G * HD), jnp.bfloat16),
            dma,
            pltpu.VMEM((chips, 2, 2 * T + 16, HD), jnp.bfloat16),
            pltpu.VMEM((2 * T + 16, HD), jnp.bfloat16),
            pltpu.VMEM((T, G * HD), jnp.bfloat16),
            pltpu.VMEM((2 * HD, G * C), jnp.bfloat16),
            pltpu.VMEM((C, C), jnp.float32),
            pltpu.VMEM((G, 1, C), jnp.float32),
            pltpu.VMEM((G, HD + 16, C), jnp.float32),
            pltpu.VMEM((G, T, HD), jnp.bfloat16),
            dma((2,)),
            dma((2,)),
            dma((Z, kinds)),
            dma((Z, kinds)),
            dma((G,)),
            dma((G,)),
        ],
        compiler_params=pltpu.CompilerParams(
            collective_id=0, has_side_effects=True, vmem_limit_bytes=53 * 1024 * 1024
        ),
    )(queries, keys_values, segment_ids.reshape(1, T))


def solution(mesh):
    in_specs = (P(("row", "col"), None), P(("row", "col"), None), P(("row", "col")))
    out_specs = P(("row", "col"), None)
    body = functools.partial(shards, n_row=mesh.shape["row"], n_col=mesh.shape["col"])
    return jax.shard_map(body, mesh=mesh, in_specs=in_specs, out_specs=out_specs, check_vma=False)
```
